512 devices in a mesh: row: 64 (over z, x), col: 8 (over y, core).
Axes of the slice: x: 4, y: 4, z: 16, core: 2. Of those that a mesh axis runs over, the one named last changes fastest.
Arguments:
- pattern: int32 [256, 16], replicated, may hold values from -1 to 255, as said below
- matrix: bfloat16 [256, 16, 128, 128], P('row', 'col'), as said below
- atom_set: int32 [4096], P('row'), may hold values from 0 to 4095, as said below
- atom_slab: int32 [4096], P('row'), may hold values from 0 to 63, as said below
- atom_offset: float32 [3, 4096], P(None, 'row'), as said below
Outputs:
- purified: float32 [256, 16, 128, 128], P('row', 'col')
- density: float32 [256, 640, 640], P('row', 'col')
The draws below stay inside these ranges and needn't reach their ends.
Inputs may be any that keep to these rules, and one draw needn't show every extreme that they name: `pattern`: entry [I, s] is -1 or a block column. The slots c * 2 to c * 2 + 1 belong to col index c and hold distinct block columns J with J mod (the number of col indices) = c. Every block row I holds its own column I. The block rows of one row index name, among the block rows of any other row index, at most one block row. `matrix`: blocks at empty slots are zero. The diagonal entries of a block at block column I of block row I lie in [0.02, 0.99]. `atom_set`: the atoms of one row index name, each once, the atom sets of that row index's block rows; atom set I * 16 + g holds orbitals g * 8 to g * 8 + 7 of block row I. `atom_slab`: an atom of row index r sits in slab r - 1, r or r + 1, taken cyclically. `atom_offset`: the first coordinate lies in [0, 4), the second in [0, 640), the third in [0, 640).
All inputs are finite; a program needn't handle non-finite values.
Results may differ from the reference program's by a relative error of at most 0.0003.
Values may be sent and summed in bfloat16 or wider, within the bound.
No kernel may reach another device: no remote copies, remote signals or barrier semaphores. Data moves between devices by JAX's collectives and lax.ppermute only.
A program may use at most 64 MiB of HBM per device.

```python
import math
import jax
import jax.numpy as jnp
from jax import lax

BS = 128
ORB = 8
SETS = 16
BR = 4
KC = 2
NB = 256
SLOTS = 16
ATOM_DEV = 64
ATOMS = 4096
PLANES = 4
GZ = 640
GX = 256
GY = 640
N_ROW = 64
N_COL = 8


def pattern_rows(key):
    key_pick, key_score = jax.random.split(key)
    allowed_count = BR + N_ROW
    owners = jnp.arange(N_ROW, dtype=jnp.int32)
    picks = jax.random.randint(key_pick, (N_ROW, N_ROW), 0, BR)
    remote = owners[None, :] * BR + picks
    remote = jnp.where(owners[None, :] == owners[:, None], -1, remote)
    local = owners[:, None] * BR + jnp.arange(BR, dtype=jnp.int32)[None, :]
    allowed = jnp.concatenate([local, remote], axis=1)
    per_row = jnp.repeat(allowed, BR, axis=0)
    row_ids = jnp.arange(NB, dtype=jnp.int32)[:, None]
    scores = jax.random.randint(key_score, (NB, allowed_count), 0, 1 << 20) * allowed_count
    scores = scores + jnp.arange(allowed_count, dtype=jnp.int32)[None, :]
    scores = jnp.where(per_row == row_ids, (1 << 21) * allowed_count, scores)
    scores = jnp.where(per_row >= 0, scores, -1)
    groups = []
    for column in range(N_COL):
        masked = jnp.where(jnp.mod(per_row, N_COL) == column, scores, -1)
        values, places = lax.top_k(masked, KC)
        chosen = jnp.take_along_axis(per_row, places, axis=1)
        groups.append(jnp.where(values >= 0, chosen, -1))
    return jnp.concatenate(groups, axis=1).astype(jnp.int32)


def draw_pattern(key, part):
    return pattern_rows(jax.random.fold_in(key, 7))


def draw_matrix(key, part):
    pattern = pattern_rows(jax.random.fold_in(key, 7))
    key_values, key_noise, key_shift = jax.random.split(jax.random.fold_in(key, 8), 3)
    scale = 2.0 / math.sqrt(SLOTS * BS)
    block_shape = (NB, SLOTS, BS, BS)
    values = jax.random.normal(key_values, block_shape, jnp.float32) * scale
    noise = 0.1 * jax.random.normal(key_noise, (NB, BS), jnp.float32)
    bottom = 0.25
    top = 0.75
    level = bottom + (top - bottom) * jnp.arange(NB).astype(jnp.float32) / (NB - 1)
    level = level + jax.random.uniform(key_shift, (), jnp.float32, -0.04, 0.04)
    diagonal = jnp.clip(level[:, None] + noise, 0.02, 0.98)
    on_diag = pattern == jnp.arange(NB, dtype=jnp.int32)[:, None]
    identity = jnp.eye(BS, dtype=bool)
    values = jnp.where(on_diag[:, :, None, None] & identity[None, None], diagonal[:, None, :, None], values)
    values = jnp.where((pattern >= 0)[:, :, None, None], values, 0.0)
    return values.astype(jnp.bfloat16)


def shuffle(row_key):
    return jax.random.permutation(row_key, ATOM_DEV)


def draw_atom_set(key, part):
    row_keys = jax.random.split(jax.random.fold_in(key, 21), N_ROW)
    orders = jax.vmap(shuffle)(row_keys).astype(jnp.int32)
    orders = orders + jnp.arange(N_ROW, dtype=jnp.int32)[:, None] * ATOM_DEV
    return orders.reshape(ATOMS)


def draw_atom_slab(key, part):
    moves = jax.random.randint(jax.random.fold_in(key, 22), (N_ROW, ATOM_DEV), -1, 2)
    slabs = jnp.mod(jnp.arange(N_ROW, dtype=jnp.int32)[:, None] + moves, N_ROW)
    return slabs.reshape(ATOMS).astype(jnp.int32)


def draw_atom_offset(key, part):
    key_x, key_y, key_z = jax.random.split(jax.random.fold_in(key, 31), 3)
    along = jax.random.uniform(key_x, (ATOMS,), jnp.float32)
    across = jax.random.uniform(key_y, (ATOMS,), jnp.float32) * GY
    depth = jax.random.uniform(key_z, (ATOMS,), jnp.float32) * GZ
    return jnp.stack([along * PLANES, across, depth])


def setup_inputs(seed: int = 0) -> dict:
    key_of = jax.random.split(jax.random.key(seed), 6)
    return {
        "pattern": draw_pattern(jax.random.fold_in(key_of[5], 71), 0),
        "matrix": draw_matrix(jax.random.fold_in(key_of[5], 71), 0),
        "atom_set": draw_atom_set(jax.random.fold_in(key_of[5], 71), 0),
        "atom_slab": draw_atom_slab(jax.random.fold_in(key_of[5], 71), 0),
        "atom_offset": draw_atom_offset(jax.random.fold_in(key_of[5], 71), 0),
    }


sharpness = 64.0
half_fill = 0.5


def window(delta, length):
    folded = jnp.mod(delta + 0.5 * length, length) - 0.5 * length
    inside = jnp.maximum(1.0 - (folded / PLANES) * (folded / PLANES), 0.0)
    return inside * inside


def collocate(near, x_cells, y_cells, z_cells, length_x, length_y, length_z):
    along_x = window(x_cells[None, :] - near[1][:, None], length_x)
    along_y = window(y_cells[None, :] - near[2][:, None], length_y)
    along_z = window(z_cells[None, :] - near[3][:, None], length_z)
    plane = near[0][:, None, None] * along_x[:, :, None] * along_y[:, None, :]
    plane = plane.reshape(near.shape[1], x_cells.shape[0] * y_cells.shape[0])
    dense = jnp.dot(plane.T, along_z, precision=lax.Precision.HIGHEST)
    return dense.reshape(x_cells.shape[0], y_cells.shape[0], z_cells.shape[0])


def reference(pattern, matrix, atom_set, atom_slab, atom_offset):
    valid = pattern >= 0
    masked = jnp.where(valid[:, :, None, None], matrix, jnp.zeros((), matrix.dtype))

    def one_row(index):
        columns = pattern[index]
        targets = jnp.where(columns >= 0, columns, 0).astype(jnp.int32)
        left = masked[index].astype(jnp.float32)
        right = masked[targets].astype(jnp.float32)
        right_columns = pattern[targets]
        matches = (right_columns[:, :, None] == columns[None, None, :]) & (columns >= 0)[:, None, None] & (columns >= 0)[None, None, :]
        terms = jnp.einsum("tab,tubc->tuac", left, right, precision=lax.Precision.HIGHEST)
        return jnp.einsum("tus,tuac->sac", matches.astype(jnp.float32), terms, precision=lax.Precision.HIGHEST)

    product = lax.map(one_row, jnp.arange(NB, dtype=jnp.int32))
    current = masked.astype(jnp.float32)
    on_diag = pattern == jnp.arange(NB, dtype=jnp.int32)[:, None]
    diag_entries = jnp.diagonal(current, axis1=2, axis2=3)
    own_diag = jnp.sum(jnp.where(on_diag[:, :, None], diag_entries, 0.0), axis=1)
    set_charge = jnp.sum(own_diag.reshape(NB * SETS, ORB), axis=1)
    trace = jnp.sum(set_charge)
    weight = jax.nn.sigmoid(sharpness * (half_fill - trace / (NB * BS)))
    purified = product + 2.0 * weight * (current - product)

    charge = set_charge[atom_set]
    start_x = atom_slab.astype(jnp.float32) * PLANES + atom_offset[0]
    stacked = jnp.stack([charge, start_x, atom_offset[1], atom_offset[2]]).reshape(4, N_ROW, ATOM_DEV)
    y_cells = jnp.arange(GY).astype(jnp.float32)
    z_cells = jnp.arange(GZ).astype(jnp.float32)

    def one_slab(slab):
        pieces = [lax.dynamic_index_in_dim(stacked, jnp.mod(slab + distance, N_ROW), 1, False) for distance in range(-2, 3)]
        near = jnp.concatenate(pieces, axis=1)
        x_cells = (slab * PLANES + jnp.arange(PLANES, dtype=jnp.int32)).astype(jnp.float32)
        return collocate(near, x_cells, y_cells, z_cells, GX, GY, GZ)

    density = lax.map(one_slab, jnp.arange(N_ROW, dtype=jnp.int32)).reshape(GX, GY, GZ)
    return purified, density
```

```python
import functools

import jax
import jax.numpy as jnp
from jax import lax
from jax.experimental import pallas as pl
from jax.experimental.pallas import tpu as pltpu
from jax.sharding import Mesh, PartitionSpec as P

ORB = 8
PLANES = 4
YC = 80
GZ = 640
NZ, NX, NY, NCORE = 16, 4, 4, 2
BR, KC, SLOTS, BS, NB = 4, 2, 16, 128, 256
CAP = 16
FULL = NZ * KC
ITEMS = BR * SLOTS * KC
ROW = ("z", "x")
COL = ("y", "core")

sharpness = 64.0
half_fill = 0.5


def shift(value, axis, steps):
    count = lax.axis_size(axis)
    return lax.ppermute(value, axis, [(s, (s + steps) % count) for s in range(count)])


def window(delta, length):
    folded = jnp.mod(delta + 0.5 * length, length) - 0.5 * length
    inside = jnp.maximum(1.0 - folded / PLANES * (folded / PLANES), 0.0)
    return inside * inside


def collocate(near, x_cells, y_cells, z_cells, length_x, length_y, length_z):
    along_x = window(x_cells[None, :] - near[1][:, None], length_x)
    along_y = window(y_cells[None, :] - near[2][:, None], length_y)
    along_z = window(z_cells[None, :] - near[3][:, None], length_z)
    plane = near[0][:, None, None] * along_x[:, :, None] * along_y[:, None, :]
    plane = plane.reshape(near.shape[1], x_cells.shape[0] * y_cells.shape[0])
    dense = jnp.dot(plane.T, along_z, precision=lax.Precision.HIGHEST)
    return dense.reshape(x_cells.shape[0], y_cells.shape[0], z_cells.shape[0])


def select_kernel(base, codes, counts, held, *rest):
    outs, sems = rest[: NX - 1], rest[NX - 1]

    def copy(d, j):
        return pltpu.make_async_copy(
            held.at[codes[d * FULL + base + j]], outs[d].at[j], sems.at[d, j]
        )

    fills = [jnp.clip(counts[d] - base, 0, CAP) for d in range(NX - 1)]
    for d in range(NX - 1):
        lax.fori_loop(0, fills[d], lambda j, _, d=d: copy(d, j).start(), None)
    for d in range(NX - 1):
        lax.fori_loop(0, fills[d], lambda j, _, d=d: copy(d, j).wait(), None)


def select(codes, counts, held, base):
    block = jax.ShapeDtypeStruct((CAP, BS, BS), jnp.bfloat16)
    return pl.pallas_call(
        functools.partial(select_kernel, base),
        out_shape=[block] * (NX - 1),
        in_specs=[
            pl.BlockSpec(memory_space=pltpu.SMEM),
            pl.BlockSpec(memory_space=pltpu.SMEM),
            pl.BlockSpec(memory_space=pl.ANY),
        ],
        out_specs=[pl.BlockSpec(memory_space=pl.ANY)] * (NX - 1),
        scratch_shapes=[pltpu.SemaphoreType.DMA((NX - 1, CAP))],
        name="select",
    )(codes, counts, held)


def product_kernel(items, count, scale, lefts, *rest):
    rights, mine, out = rest[:NX], rest[NX], rest[NX + 1]
    left_buf, right_buf, left_sem, right_sem = rest[NX + 2 :]
    total = count[0]

    def begin(n, _):
        code = items[n]
        pltpu.make_async_copy(
            lefts.at[lax.rem(code, 128)], left_buf.at[n], left_sem.at[n]
        ).start()
        source = lax.div(code, 1024)
        group = lax.div(source, 128)
        place = lax.rem(source, 128)
        for g in range(NX):

            @pl.when(group == g)
            def _():
                pltpu.make_async_copy(
                    rights[g].at[place], right_buf.at[n], right_sem.at[n]
                ).start()

    lax.fori_loop(0, total, begin, None)
    out[...] = jnp.zeros_like(out)

    def multiply(n, _):
        pltpu.make_async_copy(lefts.at[0], left_buf.at[n], left_sem.at[n]).wait()
        pltpu.make_async_copy(rights[0].at[0], right_buf.at[n], right_sem.at[n]).wait()
        target = lax.rem(lax.div(items[n], 128), 8)
        out[target] += jnp.dot(
            left_buf[n], right_buf[n], preferred_element_type=jnp.float32
        )

    lax.fori_loop(0, total, multiply, None)
    twice = scale[0]
    for o in range(BR * KC):
        value = out[o]
        out[o] = value + twice * (mine[o].astype(jnp.float32) - value)


def multiply_items(items, count, scale, lefts, rights, mine):
    smem = pl.BlockSpec(memory_space=pltpu.SMEM)
    anywhere = pl.BlockSpec(memory_space=pl.ANY)
    vmem = pl.BlockSpec(memory_space=pltpu.VMEM)
    return pl.pallas_call(
        product_kernel,
        out_shape=jax.ShapeDtypeStruct((BR * KC, BS, BS), jnp.float32),
        in_specs=[smem, smem, smem] + [anywhere] * (1 + NX) + [vmem],
        out_specs=vmem,
        scratch_shapes=[
            pltpu.VMEM((ITEMS, BS, BS), jnp.bfloat16),
            pltpu.VMEM((ITEMS, BS, BS), jnp.bfloat16),
            pltpu.SemaphoreType.DMA((ITEMS,)),
            pltpu.SemaphoreType.DMA((ITEMS,)),
        ],
        compiler_params=pltpu.CompilerParams(vmem_limit_bytes=24 * 1024 * 1024),
        name="product",
    )(items, count, scale, lefts, *rights, mine)


def compact(wanted, places, codes, slots):
    hit = wanted[..., None, :] & (places[..., None, :] == jnp.arange(slots)[:, None])
    return jnp.sum(jnp.where(hit, codes[..., None, :], 0), axis=-1)


def places_of(wanted):
    size = wanted.shape[-1]
    before = jnp.arange(size)[None, :] < jnp.arange(size)[:, None]
    return jnp.sum((wanted[..., None, :] & before).astype(jnp.int32), axis=-1)


def lookup(index, table):
    chosen = index[:, None] == jnp.arange(table.shape[0], dtype=jnp.int32)[None, :]
    found = jnp.dot(
        chosen.astype(jnp.bfloat16),
        table.astype(jnp.bfloat16),
        preferred_element_type=jnp.float32,
    )
    return found.astype(jnp.int32)


def plan(pattern, z, x, y, core):
    col = y * NCORE + core
    plane = lax.dynamic_slice_in_dim(pattern, z * NX * BR, NX * BR, 0)
    group = lax.dynamic_slice_in_dim(pattern, col * KC, KC, 1)
    targets = lax.dynamic_slice_in_dim(plane, col * KC, KC, 1)
    named = lookup(plane.reshape(-1), group).reshape(NX * BR, SLOTS, KC)
    match = (
        (named[..., None] == targets[:, None, None, :])
        & (plane >= 0)[:, :, None, None]
        & (targets >= 0)[:, None, None, :]
    )
    need = jnp.any(match, axis=-1).reshape(NX, BR * SLOTS, KC)
    refs = plane.reshape(NX, BR * SLOTS)
    owner = jnp.where(refs >= 0, refs // BR, -1)
    hit = owner[:, :, None] == jnp.arange(NZ * NX, dtype=jnp.int32)
    table = jnp.stack(
        [jnp.any(hit & need[:, :, u : u + 1], axis=1) for u in range(KC)], axis=-1
    )
    within = jnp.max(jnp.where(hit, (refs % BR)[:, :, None], 0), axis=1)
    table = table.reshape(NX, NZ, NX, KC).transpose(0, 2, 1, 3).reshape(NX, NX, FULL)
    within = within.reshape(NX, NZ, NX).transpose(0, 2, 1)
    place = places_of(table)
    counts = jnp.sum(table.astype(jnp.int32), axis=-1)
    apart = jnp.arange(NX)[:, None] != jnp.arange(NX)[None, :]
    over = jnp.sum((apart & (counts > CAP)).astype(jnp.int32))

    zs = jnp.arange(NZ, dtype=jnp.int32)[None, :, None]
    us = jnp.arange(KC, dtype=jnp.int32)[None, None, :]
    own_table = lax.dynamic_index_in_dim(table, x, 1, False)
    own_place = lax.dynamic_index_in_dim(place, x, 1, False)
    own_within = lax.dynamic_index_in_dim(within, x, 1, False)
    own_counts = lax.dynamic_index_in_dim(counts, x, 1, False)
    codes = (zs * BR + own_within[:, :, None]) * KC + us
    sends = compact(own_table, own_place, codes.reshape(NX, FULL), FULL)
    to = (x + jnp.arange(1, NX)) % NX
    pick = (to[:, None] == jnp.arange(NX)[None, :]).astype(jnp.int32)
    sends = jnp.sum(pick[:, :, None] * sends[None], axis=1)
    send_counts = jnp.sum(pick * own_counts[None], axis=1)

    my_refs = lax.dynamic_index_in_dim(refs, x, 0, False)
    my_match = lax.dynamic_slice_in_dim(match, x * BR, BR, 0)
    my_place = lax.dynamic_index_in_dim(place, x, 0, False)
    my_place = my_place.reshape(NX, NZ, KC).transpose(1, 0, 2).reshape(NZ * NX, KC)
    my_owner = jnp.maximum(my_refs, 0) // BR
    there = lookup(my_owner, my_place)
    from_x = my_owner % NX
    us = jnp.arange(KC, dtype=jnp.int32)[None, :]
    at_home = ((my_owner // NX * BR + my_refs % BR) * KC)[:, None] + us
    away = (x - from_x) % NX
    source = jnp.where((away == 0)[:, None], at_home, away[:, None] * 128 + there)
    slot = jnp.arange(SLOTS, dtype=jnp.int32)
    left_y = (y - slot // (KC * NCORE)) % NY
    left_core = slot // KC % NCORE
    rows = jnp.arange(BR, dtype=jnp.int32)[:, None]
    left = ((left_core * NY + left_y)[None, :] * BR + rows) * KC + (slot % KC)[None, :]
    wanted = jnp.any(my_match, axis=-1)
    aim = rows[:, :, None] * KC + my_match[..., 1].astype(jnp.int32)
    code = left[:, :, None] + 128 * aim + 1024 * source.reshape(BR, SLOTS, KC)
    wanted = wanted.reshape(ITEMS)
    items = compact(wanted, places_of(wanted), code.reshape(ITEMS), ITEMS)
    return (
        sends.reshape(-1),
        send_counts,
        items,
        jnp.sum(wanted.astype(jnp.int32)).reshape(1),
        over,
        targets,
    )


def shards(pattern, matrix, atom_set, atom_slab, atom_offset):
    z, x = lax.axis_index("z"), lax.axis_index("x")
    y, core = lax.axis_index("y"), lax.axis_index("core")
    row = z * NX + x
    col = y * NCORE + core
    held = lax.all_gather(matrix, "z", axis=0, tiled=True)
    held = held.reshape(NZ * BR * KC, BS, BS)

    lefts = jnp.stack([matrix] + [shift(matrix, "y", d) for d in range(1, NY)])
    lefts = lax.all_gather(lefts, "core", axis=0, tiled=False)
    lefts = lefts.reshape(NCORE * NY * BR * KC, BS, BS)

    sends, send_counts, items, count, over, plane_targets = plan(pattern, z, x, y, core)
    targets = lax.dynamic_slice_in_dim(plane_targets, x * BR, BR, 0)

    own_ids = row * BR + jnp.arange(BR, dtype=jnp.int32)
    on_diag = targets == own_ids[:, None]
    keep = on_diag[:, :, None, None] & jnp.eye(BS, dtype=bool)
    own_diag = jnp.sum(jnp.where(keep, matrix.astype(jnp.float32), 0.0), axis=(1, 2))
    sets = BS // ORB
    gather_sets = (
        jnp.arange(BS)[:, None] // ORB == jnp.arange(sets)[None, :]
    ).astype(jnp.float32)
    set_part = jnp.dot(own_diag, gather_sets, precision=lax.Precision.HIGHEST)
    packed = jnp.concatenate([set_part.reshape(-1), over.astype(jnp.float32)[None]])
    packed = lax.psum(packed, COL)
    set_charge = packed[: BR * sets]
    sums = jnp.stack([jnp.sum(set_charge), packed[BR * sets]])
    sums = lax.psum(lax.psum(sums, "x"), "z")
    weight = jax.nn.sigmoid(sharpness * (half_fill - sums[0] / (NB * BS)))
    scale = (2.0 * weight).reshape(1)

    atoms_here = atom_set.shape[0]
    find = (
        atom_set[:, None] - row * atoms_here
        == jnp.arange(atoms_here, dtype=jnp.int32)[None, :]
    ).astype(jnp.float32)
    charge = jnp.dot(find, set_charge, precision=lax.Precision.HIGHEST)
    start_x = atom_slab.astype(jnp.float32) * PLANES + atom_offset[0]
    packed = jnp.stack([charge, start_x, atom_offset[1], atom_offset[2]])
    pieces = [packed] + [shift(packed, ROW, d) for d in (1, -1, 2, -2)]
    near = jnp.concatenate(pieces, axis=1)
    x_cells = (row * PLANES + jnp.arange(PLANES, dtype=jnp.int32)).astype(jnp.float32)
    y_cells = (col * YC + jnp.arange(YC, dtype=jnp.int32)).astype(jnp.float32)
    z_cells = jnp.arange(GZ, dtype=jnp.int32).astype(jnp.float32)
    density = collocate(
        near, x_cells, y_cells, z_cells, PLANES * NZ * NX, YC * NY * NCORE, GZ
    )

    mine = matrix.reshape(BR * KC, BS, BS)
    outgoing = select(sends, send_counts, held, 0)
    first = [shift(outgoing[d - 1], "x", d) for d in range(1, NX)]

    def one_round(*first):
        return multiply_items(items, count, scale, lefts, [held, *first], mine)

    def two_rounds(*first):
        more = select(sends, send_counts, held, CAP)
        both = [
            jnp.concatenate([first[d - 1], shift(more[d - 1], "x", d)])
            for d in range(1, NX)
        ]
        return multiply_items(items, count, scale, lefts, [held, *both], mine)

    purified = lax.cond(sums[1] > 0, two_rounds, one_round, *first)
    return purified.reshape(matrix.shape), density


def solution(mesh):
    fine = Mesh(mesh.devices.reshape(NZ, NX, NY, NCORE), (*ROW, *COL))
    placed = (P(), P(ROW, COL, None, None), P(ROW), P(ROW), P(None, ROW))
    return jax.shard_map(
        shards,
        mesh=fine,
        in_specs=placed,
        out_specs=(P(ROW, COL, None, None), P(ROW, COL, None)),
        check_vma=False,
    )
```

```python
import functools

import jax
import jax.numpy as jnp
from jax import lax
from jax.experimental import pallas as pl
from jax.experimental.pallas import tpu as pltpu
from jax.sharding import Mesh, PartitionSpec as P

ORB = 8
PLANES = 4
YC = 80
GZ = 640
NZ, NX, NY, NCORE = 16, 4, 4, 2
BR, KC, SLOTS, BS, NB = 4, 2, 16, 128, 256
CAP = 12
FULL = NZ * KC
ITEMS = BR * SLOTS * KC
ROW = ("z", "x")
COL = ("y", "core")

sharpness = 64.0
half_fill = 0.5


def shift(value, axis, steps):
    count = lax.axis_size(axis)
    return lax.ppermute(value, axis, [(s, (s + steps) % count) for s in range(count)])


def window(delta, length):
    folded = jnp.mod(delta + 0.5 * length, length) - 0.5 * length
    inside = jnp.maximum(1.0 - folded / PLANES * (folded / PLANES), 0.0)
    return inside * inside


def collocate(near, x_cells, y_cells, z_cells, length_x, length_y, length_z):
    along_x = window(x_cells[None, :] - near[1][:, None], length_x)
    along_y = window(y_cells[None, :] - near[2][:, None], length_y)
    along_z = window(z_cells[None, :] - near[3][:, None], length_z)
    plane = near[0][:, None, None] * along_x[:, :, None] * along_y[:, None, :]
    plane = plane.reshape(near.shape[1], x_cells.shape[0] * y_cells.shape[0])
    dense = jnp.dot(plane.T, along_z, precision=lax.Precision.HIGHEST)
    return dense.reshape(x_cells.shape[0], y_cells.shape[0], z_cells.shape[0])


def select_kernel(base, codes, counts, held, *rest):
    outs, sems = rest[: NX - 1], rest[NX - 1]

    def copy(d, j):
        return pltpu.make_async_copy(
            held.at[codes[d * FULL + base + j]], outs[d].at[j], sems.at[d, j]
        )

    fills = [jnp.clip(counts[d] - base, 0, CAP) for d in range(NX - 1)]
    for d in range(NX - 1):
        lax.fori_loop(0, fills[d], lambda j, _, d=d: copy(d, j).start(), None)
    for d in range(NX - 1):
        lax.fori_loop(0, fills[d], lambda j, _, d=d: copy(d, j).wait(), None)


def select(codes, counts, held, base):
    block = jax.ShapeDtypeStruct((CAP, BS, BS), jnp.bfloat16)
    return pl.pallas_call(
        functools.partial(select_kernel, base),
        out_shape=[block] * (NX - 1),
        in_specs=[
            pl.BlockSpec(memory_space=pltpu.SMEM),
            pl.BlockSpec(memory_space=pltpu.SMEM),
            pl.BlockSpec(memory_space=pl.ANY),
        ],
        out_specs=[pl.BlockSpec(memory_space=pltpu.VMEM)] * (NX - 1),
        scratch_shapes=[pltpu.SemaphoreType.DMA((NX - 1, CAP))],
        name="select",
    )(codes, counts, held)


def run_items(items, total, lefts, rights, out, left_buf, right_buf, left_sem, right_sem):
    def begin(n, _):
        code = items[n]
        left = lax.rem(code, 128)
        source = lax.div(code, 1024)
        group = lax.div(source, 128)
        place = lax.rem(source, 128)
        for g in range(NCORE):

            @pl.when(lax.div(left, 32) == g)
            def _():
                pltpu.make_async_copy(
                    lefts[g].at[lax.rem(left, 32)], left_buf.at[n], left_sem.at[n]
                ).start()

        for g in range(len(rights)):

            @pl.when(group == g)
            def _():
                pltpu.make_async_copy(
                    rights[g].at[place], right_buf.at[n], right_sem.at[n]
                ).start()

    def multiply(n, _):
        pltpu.make_async_copy(lefts[0].at[0], left_buf.at[n], left_sem.at[n]).wait()
        pltpu.make_async_copy(rights[0].at[0], right_buf.at[n], right_sem.at[n]).wait()
        target = lax.rem(lax.div(items[n], 128), 8)
        out[target] += jnp.dot(
            left_buf[n], right_buf[n], preferred_element_type=jnp.float32
        )

    lax.fori_loop(0, total, begin, None)
    yield
    lax.fori_loop(0, total, multiply, None)


def home_kernel(items, count, left0, left1, held, out, *scratch):
    steps = run_items(items, count[0], (left0, left1), (held,), out, *scratch)
    next(steps)
    out[...] = jnp.zeros_like(out)
    next(steps, None)


def away_kernel(items, count, scale, left0, left1, *rest):
    rights, begun, mine, out = rest[: NX - 1], rest[NX - 1], rest[NX], rest[NX + 1]
    steps = run_items(items, count[0], (left0, left1), rights, out, *rest[NX + 2 :])
    next(steps)
    out[...] = begun[...]
    next(steps, None)
    twice = scale[0]
    for o in range(BR * KC):
        value = out[o]
        out[o] = value + twice * (mine[o].astype(jnp.float32) - value)


SMEM = pl.BlockSpec(memory_space=pltpu.SMEM)
ANYWHERE = pl.BlockSpec(memory_space=pl.ANY)
VMEM = pl.BlockSpec(memory_space=pltpu.VMEM)


def items_call(kernel, name, in_specs):
    return pl.pallas_call(
        kernel,
        out_shape=jax.ShapeDtypeStruct((BR * KC, BS, BS), jnp.float32),
        in_specs=in_specs,
        out_specs=VMEM,
        scratch_shapes=[
            pltpu.VMEM((ITEMS, BS, BS), jnp.bfloat16),
            pltpu.VMEM((ITEMS, BS, BS), jnp.bfloat16),
            pltpu.SemaphoreType.DMA((ITEMS,)),
            pltpu.SemaphoreType.DMA((ITEMS,)),
        ],
        compiler_params=pltpu.CompilerParams(vmem_limit_bytes=24 * 1024 * 1024),
        cost_estimate=pl.CostEstimate(
            flops=2 * 16 * BS**3, bytes_accessed=16 * 4 * BS * BS, transcendentals=0
        ),
        name=name,
    )


def home_products(items, count, lefts, held):
    call = items_call(home_kernel, "home", [SMEM] * 2 + [ANYWHERE] * 3)
    return call(items, count, *lefts, held)


def away_products(items, count, scale, lefts, rights, begun, mine):
    specs = [SMEM] * 3 + [ANYWHERE] * (NX + 1) + [VMEM] * 2
    call = items_call(away_kernel, "away", specs)
    return call(items, count, scale, *lefts, *rights, begun, mine)


def compact(wanted, places, codes, slots):
    hit = wanted[..., None, :] & (places[..., None, :] == jnp.arange(slots)[:, None])
    return jnp.sum(jnp.where(hit, codes[..., None, :], 0), axis=-1)


def places_of(wanted):
    size = wanted.shape[-1]
    before = jnp.arange(size)[None, :] < jnp.arange(size)[:, None]
    return jnp.sum((wanted[..., None, :] & before).astype(jnp.int32), axis=-1)


def lookup(index, table):
    chosen = index[:, None] == jnp.arange(table.shape[0], dtype=jnp.int32)[None, :]
    found = jnp.dot(
        chosen.astype(jnp.bfloat16),
        table.astype(jnp.bfloat16),
        preferred_element_type=jnp.float32,
    )
    return found.astype(jnp.int32)


def plan(pattern, z, x, y, core):
    col = y * NCORE + core
    plane = lax.dynamic_slice_in_dim(pattern, z * NX * BR, NX * BR, 0)
    group = lax.dynamic_slice_in_dim(pattern, col * KC, KC, 1)
    targets = lax.dynamic_slice_in_dim(plane, col * KC, KC, 1)
    named = lookup(plane.reshape(-1), group).reshape(NX * BR, SLOTS, KC)
    match = (
        (named[..., None] == targets[:, None, None, :])
        & (plane >= 0)[:, :, None, None]
        & (targets >= 0)[:, None, None, :]
    )
    need = jnp.any(match, axis=-1).reshape(NX, BR * SLOTS, KC)
    refs = plane.reshape(NX, BR * SLOTS)
    owner = jnp.where(refs >= 0, refs // BR, -1)
    hit = owner[:, :, None] == jnp.arange(NZ * NX, dtype=jnp.int32)
    table = jnp.stack(
        [jnp.any(hit & need[:, :, u : u + 1], axis=1) for u in range(KC)], axis=-1
    )
    within = jnp.max(jnp.where(hit, (refs % BR)[:, :, None], 0), axis=1)
    table = table.reshape(NX, NZ, NX, KC).transpose(0, 2, 1, 3).reshape(NX, NX, FULL)
    within = within.reshape(NX, NZ, NX).transpose(0, 2, 1)
    place = places_of(table)
    counts = jnp.sum(table.astype(jnp.int32), axis=-1)
    apart = jnp.arange(NX)[:, None] != jnp.arange(NX)[None, :]
    over = jnp.sum((apart & (counts > CAP)).astype(jnp.int32))

    zs = jnp.arange(NZ, dtype=jnp.int32)[None, :, None]
    us = jnp.arange(KC, dtype=jnp.int32)[None, None, :]
    own_table = lax.dynamic_index_in_dim(table, x, 1, False)
    own_place = lax.dynamic_index_in_dim(place, x, 1, False)
    own_within = lax.dynamic_index_in_dim(within, x, 1, False)
    own_counts = lax.dynamic_index_in_dim(counts, x, 1, False)
    codes = (zs * BR + own_within[:, :, None]) * KC + us
    sends = compact(own_table, own_place, codes.reshape(NX, FULL), FULL)
    to = (x + jnp.arange(1, NX)) % NX
    pick = (to[:, None] == jnp.arange(NX)[None, :]).astype(jnp.int32)
    sends = jnp.sum(pick[:, :, None] * sends[None], axis=1)
    send_counts = jnp.sum(pick * own_counts[None], axis=1)

    my_refs = lax.dynamic_index_in_dim(refs, x, 0, False)
    my_match = lax.dynamic_slice_in_dim(match, x * BR, BR, 0)
    my_place = lax.dynamic_index_in_dim(place, x, 0, False)
    my_place = my_place.reshape(NX, NZ, KC).transpose(1, 0, 2).reshape(NZ * NX, KC)
    my_owner = jnp.maximum(my_refs, 0) // BR
    there = lookup(my_owner, my_place)
    from_x = my_owner % NX
    us = jnp.arange(KC, dtype=jnp.int32)[None, :]
    at_home = ((my_owner // NX * BR + my_refs % BR) * KC)[:, None] + us
    away = (x - from_x) % NX
    source = jnp.where((away == 0)[:, None], at_home, (away[:, None] - 1) * 128 + there)
    slot = jnp.arange(SLOTS, dtype=jnp.int32)
    left_y = (y - slot // (KC * NCORE)) % NY
    left_core = (slot // KC + core) % NCORE
    rows = jnp.arange(BR, dtype=jnp.int32)[:, None]
    left = ((left_core * NY + left_y)[None, :] * BR + rows) * KC + (slot % KC)[None, :]
    wanted = jnp.any(my_match, axis=-1)
    aim = rows[:, :, None] * KC + my_match[..., 1].astype(jnp.int32)
    code = left[:, :, None] + 128 * aim + 1024 * source.reshape(BR, SLOTS, KC)
    wanted = wanted & jnp.stack([away == 0, away > 0]).reshape(2, BR, SLOTS, 1)
    wanted = wanted.reshape(2, ITEMS)
    items = compact(wanted, places_of(wanted), code.reshape(1, ITEMS), ITEMS)
    totals = jnp.sum(wanted.astype(jnp.int32), axis=-1)
    return sends.reshape(-1), send_counts, items, totals, over, targets


def shards(pattern, matrix, atom_set, atom_slab, atom_offset):
    z, x = lax.axis_index("z"), lax.axis_index("x")
    y, core = lax.axis_index("y"), lax.axis_index("core")
    row = z * NX + x
    col = y * NCORE + core
    held = lax.all_gather(matrix, "z", axis=0, tiled=True)
    held = held.reshape(NZ * BR * KC, BS, BS)

    sends, send_counts, items, totals, over, plane_targets = plan(pattern, z, x, y, core)
    targets = lax.dynamic_slice_in_dim(plane_targets, x * BR, BR, 0)

    own_ids = row * BR + jnp.arange(BR, dtype=jnp.int32)
    on_diag = targets == own_ids[:, None]
    keep = on_diag[:, :, None, None] & jnp.eye(BS, dtype=bool)
    own_diag = jnp.sum(jnp.where(keep, matrix.astype(jnp.float32), 0.0), axis=(1, 2))
    sets = BS // ORB
    gather_sets = (
        jnp.arange(BS)[:, None] // ORB == jnp.arange(sets)[None, :]
    ).astype(jnp.float32)
    set_part = jnp.dot(own_diag, gather_sets, precision=lax.Precision.HIGHEST)
    packed = jnp.concatenate([set_part.reshape(-1), over.astype(jnp.float32)[None]])
    packed = lax.psum(packed, COL)
    blocks, packed = lax.optimization_barrier((matrix, packed))
    lefts = jnp.concatenate([blocks] + [shift(blocks, "y", d) for d in range(1, NY)])
    lefts = lefts.reshape(NY * BR * KC, BS, BS)
    lefts = (lefts, shift(lefts, "core", 1))
    set_charge = packed[: BR * sets]

    atoms_here = atom_set.shape[0]
    find = (
        atom_set[:, None] - row * atoms_here
        == jnp.arange(atoms_here, dtype=jnp.int32)[None, :]
    ).astype(jnp.float32)
    charge = jnp.dot(find, set_charge, precision=lax.Precision.HIGHEST)
    start_x = atom_slab.astype(jnp.float32) * PLANES + atom_offset[0]
    flag = jnp.broadcast_to(packed[BR * sets], charge.shape)
    packed = jnp.stack([charge, start_x, atom_offset[1], atom_offset[2], flag])
    packed = lax.all_gather(packed, "x", axis=0, tiled=False)
    packed = lax.all_gather(packed, "z", axis=0, tiled=False)
    packed = packed.reshape(NZ * NX, 5, atoms_here)
    over = jnp.sum(packed[:, 4, 0])
    trace = jnp.sum(packed[:, 0])
    weight = jax.nn.sigmoid(sharpness * (half_fill - trace / (NB * BS)))
    scale = (2.0 * weight).reshape(1)
    packed = jnp.concatenate([packed[-2:], packed, packed[:2]])
    near = lax.dynamic_slice_in_dim(packed, row, 5, 0)[:, :4]
    near = near.transpose(1, 0, 2).reshape(4, 5 * atoms_here)

    mine = matrix.reshape(BR * KC, BS, BS)
    outgoing = select(sends, send_counts, held, 0)
    items, near, outgoing = lax.optimization_barrier((items, near, outgoing))
    first = [shift(outgoing[d - 1], "x", d) for d in range(1, NX)]
    begun = home_products(items[0], totals[:1], lefts, held)

    x_cells = (row * PLANES + jnp.arange(PLANES, dtype=jnp.int32)).astype(jnp.float32)
    y_cells = (col * YC + jnp.arange(YC, dtype=jnp.int32)).astype(jnp.float32)
    z_cells = jnp.arange(GZ, dtype=jnp.int32).astype(jnp.float32)
    density = collocate(
        near, x_cells, y_cells, z_cells, PLANES * NZ * NX, YC * NY * NCORE, GZ
    )

    def finish(rights):
        return away_products(items[1], totals[1:], scale, lefts, rights, begun, mine)

    def one_round(*first):
        return finish(first)

    def two_rounds(*first):
        both = list(first)
        for base in range(CAP, FULL, CAP):
            more = select(sends, send_counts, held, base)
            for d in range(1, NX):
                coming = shift(more[d - 1], "x", d)
                both[d - 1] = jnp.concatenate([both[d - 1], coming])
        return finish(both)

    purified = lax.cond(over > 0, two_rounds, one_round, *first)
    return purified.reshape(matrix.shape), density


def solution(mesh):
    fine = Mesh(mesh.devices.reshape(NZ, NX, NY, NCORE), (*ROW, *COL))
    placed = (P(), P(ROW, COL, None, None), P(ROW), P(ROW), P(None, ROW))
    return jax.shard_map(
        shards,
        mesh=fine,
        in_specs=placed,
        out_specs=(P(ROW, COL, None, None), P(ROW, COL, None)),
        check_vma=False,
    )
```

```python
import functools

import jax
import jax.numpy as jnp
from jax import lax
from jax.experimental import pallas as pl
from jax.experimental.pallas import tpu as pltpu
from jax.sharding import Mesh, PartitionSpec as P

ORB = 8
PLANES = 4
YC = 80
GZ = 640
NZ, NX, NY, NCORE = 16, 4, 4, 2
BR, KC, SLOTS, BS, NB = 4, 2, 16, 128, 256
CAP = 12
FULL = NZ * KC
ITEMS = BR * SLOTS * KC
GROUP = 4
SUMS = BR * KC + 1
ROW = ("z", "x")
COL = ("y", "core")

sharpness = 64.0
half_fill = 0.5


def shift(value, axis, steps):
    count = lax.axis_size(axis)
    return lax.ppermute(value, axis, [(s, (s + steps) % count) for s in range(count)])


def everyone(value, axis):
    count = lax.axis_size(axis)
    spread = jnp.broadcast_to(value[None], (count, *value.shape))
    return lax.all_to_all(spread, axis, split_axis=0, concat_axis=0, tiled=True)


def window(delta, length):
    folded = jnp.mod(delta + 0.5 * length, length) - 0.5 * length
    inside = jnp.maximum(1.0 - folded / PLANES * (folded / PLANES), 0.0)
    return inside * inside


def collocate(near, x_cells, y_cells, z_cells, length_x, length_y, length_z):
    along_x = window(x_cells[None, :] - near[1][:, None], length_x)
    along_y = window(y_cells[None, :] - near[2][:, None], length_y)
    along_z = window(z_cells[None, :] - near[3][:, None], length_z)
    plane = near[0][:, None, None] * along_x[:, :, None] * along_y[:, None, :]
    plane = plane.reshape(near.shape[1], x_cells.shape[0] * y_cells.shape[0])
    dense = jnp.dot(plane.T, along_z, precision=lax.Precision.HIGHEST)
    return dense.reshape(x_cells.shape[0], y_cells.shape[0], z_cells.shape[0])


def select_kernel(base, codes, counts, held, *rest):
    outs, sems = rest[: NX - 1], rest[NX - 1]

    def copy(d, j):
        return pltpu.make_async_copy(
            held.at[codes[d * FULL + base + j]], outs[d].at[j], sems.at[d, j]
        )

    fills = [jnp.clip(counts[d] - base, 0, CAP) for d in range(NX - 1)]
    for d in range(NX - 1):
        lax.fori_loop(0, fills[d], lambda j, _, d=d: copy(d, j).start(), None)
    for d in range(NX - 1):
        lax.fori_loop(0, fills[d], lambda j, _, d=d: copy(d, j).wait(), None)


def select(codes, counts, held, base):
    block = jax.ShapeDtypeStruct((CAP, BS, BS), jnp.bfloat16)
    return pl.pallas_call(
        functools.partial(select_kernel, base),
        out_shape=[block] * (NX - 1),
        in_specs=[
            pl.BlockSpec(memory_space=pltpu.SMEM),
            pl.BlockSpec(memory_space=pltpu.SMEM),
            pl.BlockSpec(memory_space=pl.ANY),
        ],
        out_specs=[pl.BlockSpec(memory_space=pltpu.VMEM)] * (NX - 1),
        scratch_shapes=[pltpu.SemaphoreType.DMA((NX - 1, CAP))],
        name="select",
    )(codes, counts, held)


def run_items(items, total, lefts, rights, sums, left_buf, right_buf, left_sem, right_sem):
    def begin(n, _):
        code = items[n]
        left = lax.rem(code, 128)
        source = lax.div(code, 1024)
        group = lax.div(source, 128)
        place = lax.rem(source, 128)
        for g in range(NCORE):

            @pl.when(lax.div(left, 32) == g)
            def _():
                pltpu.make_async_copy(
                    lefts[g].at[lax.rem(left, 32)], left_buf.at[n], left_sem.at[n]
                ).start()

        for g in range(len(rights)):

            @pl.when(group == g)
            def _():
                pltpu.make_async_copy(
                    rights[g].at[place], right_buf.at[n], right_sem.at[n]
                ).start()

    def multiply(q, _):
        places = [q * GROUP + k for k in range(GROUP)]
        for n in places:

            @pl.when(n < total)
            def _():
                pltpu.make_async_copy(
                    lefts[0].at[0], left_buf.at[n], left_sem.at[n]
                ).wait()
                pltpu.make_async_copy(
                    rights[0].at[0], right_buf.at[n], right_sem.at[n]
                ).wait()

        terms = [
            jnp.dot(left_buf[n], right_buf[n], preferred_element_type=jnp.float32)
            for n in places
        ]
        for n, term in zip(places, terms):
            target = lax.rem(lax.div(items[n], 128), 8)
            sums[jnp.where(n < total, target, BR * KC)] += term

    lax.fori_loop(0, total, begin, None)
    yield
    lax.fori_loop(0, lax.div(total + GROUP - 1, GROUP), multiply, None)


def home_kernel(items, count, left0, left1, held, sums, *scratch):
    steps = run_items(items, count[0], (left0, left1), (held,), sums, *scratch)
    next(steps)
    sums[...] = jnp.zeros_like(sums)
    next(steps, None)


def away_kernel(items, count, scale, left0, left1, *rest):
    rights, begun, mine, out = rest[: NX - 1], rest[NX - 1], rest[NX], rest[NX + 1]
    *scratch, sums = rest[NX + 2 :]
    steps = run_items(items, count[0], (left0, left1), rights, sums, *scratch)
    next(steps)
    sums[...] = begun[...]
    next(steps, None)
    twice = scale[0]
    for o in range(BR * KC):
        value = sums[o]
        out[o] = value + twice * (mine[o].astype(jnp.float32) - value)


SMEM = pl.BlockSpec(memory_space=pltpu.SMEM)
ANYWHERE = pl.BlockSpec(memory_space=pl.ANY)
VMEM = pl.BlockSpec(memory_space=pltpu.VMEM)


def items_call(kernel, name, in_specs, size, more):
    return pl.pallas_call(
        kernel,
        out_shape=jax.ShapeDtypeStruct((size, BS, BS), jnp.float32),
        in_specs=in_specs,
        out_specs=VMEM,
        scratch_shapes=[
            pltpu.VMEM((ITEMS, BS, BS), jnp.bfloat16),
            pltpu.VMEM((ITEMS, BS, BS), jnp.bfloat16),
            pltpu.SemaphoreType.DMA((ITEMS,)),
            pltpu.SemaphoreType.DMA((ITEMS,)),
            *more,
        ],
        compiler_params=pltpu.CompilerParams(vmem_limit_bytes=24 * 1024 * 1024),
        cost_estimate=pl.CostEstimate(
            flops=2 * 16 * BS**3, bytes_accessed=16 * 4 * BS * BS, transcendentals=0
        ),
        name=name,
    )


def home_products(items, count, lefts, held):
    call = items_call(home_kernel, "home", [SMEM] * 2 + [ANYWHERE] * 3, SUMS, [])
    return call(items, count, *lefts, held)


def away_products(items, count, scale, lefts, rights, begun, mine):
    specs = [SMEM] * 3 + [ANYWHERE] * (NX + 1) + [VMEM] * 2
    sums = pltpu.VMEM((SUMS, BS, BS), jnp.float32)
    call = items_call(away_kernel, "away", specs, BR * KC, [sums])
    return call(items, count, scale, *lefts, *rights, begun, mine)


def compact(wanted, places, codes, slots):
    hit = wanted[..., None, :] & (places[..., None, :] == jnp.arange(slots)[:, None])
    return jnp.sum(jnp.where(hit, codes[..., None, :], 0), axis=-1)


def places_of(wanted):
    size = wanted.shape[-1]
    before = jnp.arange(size)[None, :] < jnp.arange(size)[:, None]
    return jnp.sum((wanted[..., None, :] & before).astype(jnp.int32), axis=-1)


def lookup(index, table):
    chosen = index[:, None] == jnp.arange(table.shape[0], dtype=jnp.int32)[None, :]
    found = jnp.dot(
        chosen.astype(jnp.bfloat16),
        table.astype(jnp.bfloat16),
        preferred_element_type=jnp.float32,
    )
    return found.astype(jnp.int32)


def plan(pattern, z, x, y, core):
    col = y * NCORE + core
    plane = lax.dynamic_slice_in_dim(pattern, z * NX * BR, NX * BR, 0)
    group = lax.dynamic_slice_in_dim(pattern, col * KC, KC, 1)
    targets = lax.dynamic_slice_in_dim(plane, col * KC, KC, 1)
    named = lookup(plane.reshape(-1), group).reshape(NX * BR, SLOTS, KC)
    match = (
        (named[..., None] == targets[:, None, None, :])
        & (plane >= 0)[:, :, None, None]
        & (targets >= 0)[:, None, None, :]
    )
    need = jnp.any(match, axis=-1).reshape(NX, BR * SLOTS, KC)
    refs = plane.reshape(NX, BR * SLOTS)
    owner = jnp.where(refs >= 0, refs // BR, -1)
    hit = owner[:, :, None] == jnp.arange(NZ * NX, dtype=jnp.int32)
    table = jnp.stack(
        [jnp.any(hit & need[:, :, u : u + 1], axis=1) for u in range(KC)], axis=-1
    )
    within = jnp.max(jnp.where(hit, (refs % BR)[:, :, None], 0), axis=1)
    table = table.reshape(NX, NZ, NX, KC).transpose(0, 2, 1, 3).reshape(NX, NX, FULL)
    within = within.reshape(NX, NZ, NX).transpose(0, 2, 1)
    place = places_of(table)
    counts = jnp.sum(table.astype(jnp.int32), axis=-1)
    apart = jnp.arange(NX)[:, None] != jnp.arange(NX)[None, :]
    over = jnp.sum((apart & (counts > CAP)).astype(jnp.int32))

    zs = jnp.arange(NZ, dtype=jnp.int32)[None, :, None]
    us = jnp.arange(KC, dtype=jnp.int32)[None, None, :]
    own_table = lax.dynamic_index_in_dim(table, x, 1, False)
    own_place = lax.dynamic_index_in_dim(place, x, 1, False)
    own_within = lax.dynamic_index_in_dim(within, x, 1, False)
    own_counts = lax.dynamic_index_in_dim(counts, x, 1, False)
    codes = (zs * BR + own_within[:, :, None]) * KC + us
    sends = compact(own_table, own_place, codes.reshape(NX, FULL), FULL)
    to = (x + jnp.arange(1, NX)) % NX
    pick = (to[:, None] == jnp.arange(NX)[None, :]).astype(jnp.int32)
    sends = jnp.sum(pick[:, :, None] * sends[None], axis=1)
    send_counts = jnp.sum(pick * own_counts[None], axis=1)

    my_refs = lax.dynamic_index_in_dim(refs, x, 0, False)
    my_match = lax.dynamic_slice_in_dim(match, x * BR, BR, 0)
    my_place = lax.dynamic_index_in_dim(place, x, 0, False)
    my_place = my_place.reshape(NX, NZ, KC).transpose(1, 0, 2).reshape(NZ * NX, KC)
    my_owner = jnp.maximum(my_refs, 0) // BR
    there = lookup(my_owner, my_place)
    from_x = my_owner % NX
    us = jnp.arange(KC, dtype=jnp.int32)[None, :]
    at_home = ((my_owner // NX * BR + my_refs % BR) * KC)[:, None] + us
    away = (x - from_x) % NX
    source = jnp.where((away == 0)[:, None], at_home, (away[:, None] - 1) * 128 + there)
    slot = jnp.arange(SLOTS, dtype=jnp.int32)
    left_y = (y - slot // (KC * NCORE)) % NY
    left_core = (slot // KC + core) % NCORE
    rows = jnp.arange(BR, dtype=jnp.int32)[:, None]
    left = ((left_core * NY + left_y)[None, :] * BR + rows) * KC + (slot % KC)[None, :]
    wanted = jnp.any(my_match, axis=-1)
    aim = rows[:, :, None] * KC + my_match[..., 1].astype(jnp.int32)
    code = left[:, :, None] + 128 * aim + 1024 * source.reshape(BR, SLOTS, KC)
    wanted = wanted & jnp.stack([away == 0, away > 0]).reshape(2, BR, SLOTS, 1)
    wanted = wanted.reshape(2, ITEMS)
    items = compact(wanted, places_of(wanted), code.reshape(1, ITEMS), ITEMS)
    totals = jnp.sum(wanted.astype(jnp.int32), axis=-1)
    return sends.reshape(-1), send_counts, items, totals, over, targets


def shards(pattern, matrix, atom_set, atom_slab, atom_offset):
    z, x = lax.axis_index("z"), lax.axis_index("x")
    y, core = lax.axis_index("y"), lax.axis_index("core")
    row = z * NX + x
    col = y * NCORE + core
    held = lax.all_gather(matrix, "z", axis=0, tiled=True)
    held = held.reshape(NZ * BR * KC, BS, BS)

    sends, send_counts, items, totals, over, plane_targets = plan(pattern, z, x, y, core)
    targets = lax.dynamic_slice_in_dim(plane_targets, x * BR, BR, 0)

    own_ids = row * BR + jnp.arange(BR, dtype=jnp.int32)
    on_diag = targets == own_ids[:, None]
    keep = on_diag[:, :, None, None] & jnp.eye(BS, dtype=bool)
    own_diag = jnp.sum(jnp.where(keep, matrix.astype(jnp.float32), 0.0), axis=(1, 2))
    sets = BS // ORB
    gather_sets = (
        jnp.arange(BS)[:, None] // ORB == jnp.arange(sets)[None, :]
    ).astype(jnp.float32)
    set_part = jnp.dot(own_diag, gather_sets, precision=lax.Precision.HIGHEST)
    packed = jnp.concatenate([set_part.reshape(-1), over.astype(jnp.float32)[None]])
    packed = jnp.sum(everyone(packed[None], COL), axis=0)[0]
    blocks, packed = lax.optimization_barrier((matrix, packed))
    lefts = jnp.concatenate([blocks] + [shift(blocks, "y", d) for d in range(1, NY)])
    lefts = lefts.reshape(NY * BR * KC, BS, BS)
    lefts = (lefts, shift(lefts, "core", 1))
    set_charge = packed[: BR * sets]

    atoms_here = atom_set.shape[0]
    find = (
        atom_set[:, None] - row * atoms_here
        == jnp.arange(atoms_here, dtype=jnp.int32)[None, :]
    ).astype(jnp.float32)
    charge = jnp.dot(find, set_charge, precision=lax.Precision.HIGHEST)
    start_x = atom_slab.astype(jnp.float32) * PLANES + atom_offset[0]
    flag = jnp.broadcast_to(packed[BR * sets], charge.shape)
    packed = jnp.stack([charge, start_x, atom_offset[1], atom_offset[2], flag])
    packed = everyone(packed, ROW)
    over = jnp.sum(packed[:, 4, 0])
    trace = jnp.sum(packed[:, 0])
    weight = jax.nn.sigmoid(sharpness * (half_fill - trace / (NB * BS)))
    scale = (2.0 * weight).reshape(1)
    packed = jnp.concatenate([packed[-2:], packed, packed[:2]])
    near = lax.dynamic_slice_in_dim(packed, row, 5, 0)[:, :4]
    near = near.transpose(1, 0, 2).reshape(4, 5 * atoms_here)

    mine = matrix.reshape(BR * KC, BS, BS)
    outgoing = select(sends, send_counts, held, 0)
    first = [None] * (NX - 1)
    for d in (2, 3, 1):
        items, outgoing = lax.optimization_barrier((items, outgoing))
        first[d - 1] = shift(outgoing[d - 1], "x", d)
    begun = home_products(items[0], totals[:1], lefts, held)

    x_cells = (row * PLANES + jnp.arange(PLANES, dtype=jnp.int32)).astype(jnp.float32)
    y_cells = (col * YC + jnp.arange(YC, dtype=jnp.int32)).astype(jnp.float32)
    z_cells = jnp.arange(GZ, dtype=jnp.int32).astype(jnp.float32)
    density = collocate(
        near, x_cells, y_cells, z_cells, PLANES * NZ * NX, YC * NY * NCORE, GZ
    )

    def finish(rights):
        return away_products(items[1], totals[1:], scale, lefts, rights, begun, mine)

    def one_round(*first):
        return finish(first)

    def two_rounds(*first):
        both = list(first)
        for base in range(CAP, FULL, CAP):
            more = select(sends, send_counts, held, base)
            for d in range(1, NX):
                coming = shift(more[d - 1], "x", d)
                both[d - 1] = jnp.concatenate([both[d - 1], coming])
        return finish(both)

    purified = lax.cond(over > 0, two_rounds, one_round, *first)
    return purified.reshape(matrix.shape), density


def solution(mesh):
    fine = Mesh(mesh.devices.reshape(NZ, NX, NY, NCORE), (*ROW, *COL))
    placed = (P(), P(ROW, COL, None, None), P(ROW), P(ROW), P(None, ROW))
    return jax.shard_map(
        shards,
        mesh=fine,
        in_specs=placed,
        out_specs=(P(ROW, COL, None, None), P(ROW, COL, None)),
        check_vma=False,
    )
```

```python
import functools

import jax
import jax.numpy as jnp
from jax import lax
from jax.experimental import pallas as pl
from jax.experimental.pallas import tpu as pltpu
from jax.sharding import Mesh, PartitionSpec as P

ORB = 8
PLANES = 4
YC = 80
GZ = 640
NZ, NX, NY, NCORE = 16, 4, 4, 2
BR, KC, SLOTS, BS, NB = 4, 2, 16, 128, 256
CAP = 12
FULL = NZ * KC
ITEMS = BR * SLOTS * KC
GROUP = 4
SUMS = BR * KC + 1
ROW = ("z", "x")
COL = ("y", "core")

sharpness = 64.0
half_fill = 0.5


def shift(value, axis, steps):
    count = lax.axis_size(axis)
    return lax.ppermute(value, axis, [(s, (s + steps) % count) for s in range(count)])


def exchange(value, axis):
    return lax.all_to_all(value, axis, split_axis=0, concat_axis=0, tiled=True)


def everyone(value, axis):
    count = lax.axis_size(axis)
    spread = jnp.broadcast_to(value[None], (count, *value.shape))
    return exchange(spread, axis)


def window(delta, length):
    folded = jnp.mod(delta + 0.5 * length, length) - 0.5 * length
    inside = jnp.maximum(1.0 - folded / PLANES * (folded / PLANES), 0.0)
    return inside * inside


def collocate(near, x_cells, y_cells, z_cells, length_x, length_y, length_z):
    along_x = window(x_cells[None, :] - near[1][:, None], length_x)
    along_y = window(y_cells[None, :] - near[2][:, None], length_y)
    along_z = window(z_cells[None, :] - near[3][:, None], length_z)
    plane = near[0][:, None, None] * along_x[:, :, None] * along_y[:, None, :]
    plane = plane.reshape(near.shape[1], x_cells.shape[0] * y_cells.shape[0])
    dense = jnp.dot(plane.T, along_z, precision=lax.Precision.HIGHEST)
    return dense.reshape(x_cells.shape[0], y_cells.shape[0], z_cells.shape[0])


SMEM = pl.BlockSpec(memory_space=pltpu.SMEM)
ANYWHERE = pl.BlockSpec(memory_space=pl.ANY)
VMEM = pl.BlockSpec(memory_space=pltpu.VMEM)


def select_kernel(base, codes, counts, held, out, sems):
    def copy(d, j):
        return pltpu.make_async_copy(
            held.at[codes[d * FULL + base + j]], out.at[d, j], sems.at[d, j]
        )

    fills = [jnp.clip(counts[d] - base, 0, CAP) for d in range(NX)]
    for d in range(NX):
        lax.fori_loop(0, fills[d], lambda j, _, d=d: copy(d, j).start(), None)
    for d in range(NX):
        lax.fori_loop(0, fills[d], lambda j, _, d=d: copy(d, j).wait(), None)


def select(codes, counts, held, base):
    return pl.pallas_call(
        functools.partial(select_kernel, base),
        out_shape=jax.ShapeDtypeStruct((NX, CAP, BS, BS), jnp.bfloat16),
        in_specs=[SMEM, SMEM, ANYWHERE],
        out_specs=VMEM,
        scratch_shapes=[pltpu.SemaphoreType.DMA((NX, CAP))],
        name="select",
    )(codes, counts, held)


def run_items(items, total, lefts, rights, stride, sums):
    def multiply(q, _):
        codes = [items[q * GROUP + k] for k in range(GROUP)]
        terms = [
            jnp.dot(
                lefts[code & 127],
                rights[((code >> 10) & 127) + (code >> 17) * stride],
                preferred_element_type=jnp.float32,
            )
            for code in codes
        ]
        for k, (code, term) in enumerate(zip(codes, terms)):
            target = (code >> 7) & 7
            sums[jnp.where(q * GROUP + k < total, target, BR * KC)] += term

    lax.fori_loop(0, lax.div(total + GROUP - 1, GROUP), multiply, None)


def home_kernel(items, count, lefts, held, sums):
    sums[...] = jnp.zeros_like(sums)
    run_items(items, count[0], lefts, held, 0, sums)


def away_kernel(items, count, scale, lefts, rights, begun, mine, out, sums):
    sums[...] = begun[...]
    run_items(items, count[0], lefts, rights, rights.shape[0] // NX, sums)
    twice = scale[0]
    for o in range(BR * KC):
        value = sums[o]
        out[o] = value + twice * (mine[o].astype(jnp.float32) - value)


def items_call(kernel, name, in_specs, size, scratch):
    return pl.pallas_call(
        kernel,
        out_shape=jax.ShapeDtypeStruct((size, BS, BS), jnp.float32),
        in_specs=in_specs,
        out_specs=VMEM,
        scratch_shapes=scratch,
        compiler_params=pltpu.CompilerParams(vmem_limit_bytes=24 * 1024 * 1024),
        cost_estimate=pl.CostEstimate(
            flops=2 * 16 * BS**3, bytes_accessed=6 << 20, transcendentals=0
        ),
        name=name,
    )


def home_products(items, count, lefts, held):
    call = items_call(home_kernel, "home", [SMEM] * 2 + [VMEM] * 2, SUMS, [])
    return call(items, count, lefts, held)


def away_products(items, count, scale, lefts, rights, begun, mine):
    specs = [SMEM] * 3 + [VMEM] * 4
    sums = pltpu.VMEM((SUMS, BS, BS), jnp.float32)
    call = items_call(away_kernel, "away", specs, BR * KC, [sums])
    return call(items, count, scale, lefts, rights, begun, mine)


def compact(wanted, places, codes, slots):
    hit = wanted[..., None, :] & (places[..., None, :] == jnp.arange(slots)[:, None])
    return jnp.sum(jnp.where(hit, codes[..., None, :], 0), axis=-1)


def places_of(wanted):
    size = wanted.shape[-1]
    before = jnp.arange(size)[None, :] < jnp.arange(size)[:, None]
    return jnp.sum((wanted[..., None, :] & before).astype(jnp.int32), axis=-1)


def lookup(index, table):
    chosen = index[:, None] == jnp.arange(table.shape[0], dtype=jnp.int32)[None, :]
    found = jnp.dot(
        chosen.astype(jnp.bfloat16),
        table.astype(jnp.bfloat16),
        preferred_element_type=jnp.float32,
    )
    return found.astype(jnp.int32)


def plan(pattern, z, x, y, core):
    col = y * NCORE + core
    plane = lax.dynamic_slice_in_dim(pattern, z * NX * BR, NX * BR, 0)
    group = lax.dynamic_slice_in_dim(pattern, col * KC, KC, 1)
    targets = lax.dynamic_slice_in_dim(plane, col * KC, KC, 1)
    named = lookup(plane.reshape(-1), group).reshape(NX * BR, SLOTS, KC)
    match = (
        (named[..., None] == targets[:, None, None, :])
        & (plane >= 0)[:, :, None, None]
        & (targets >= 0)[:, None, None, :]
    )
    need = jnp.any(match, axis=-1).reshape(NX, BR * SLOTS, KC)
    refs = plane.reshape(NX, BR * SLOTS)
    owner = jnp.where(refs >= 0, refs // BR, -1)
    hit = owner[:, :, None] == jnp.arange(NZ * NX, dtype=jnp.int32)
    table = jnp.stack(
        [jnp.any(hit & need[:, :, u : u + 1], axis=1) for u in range(KC)], axis=-1
    )
    within = jnp.max(jnp.where(hit, (refs % BR)[:, :, None], 0), axis=1)
    table = table.reshape(NX, NZ, NX, KC).transpose(0, 2, 1, 3).reshape(NX, NX, FULL)
    within = within.reshape(NX, NZ, NX).transpose(0, 2, 1)
    place = places_of(table)
    counts = jnp.sum(table.astype(jnp.int32), axis=-1)
    apart = jnp.arange(NX)[:, None] != jnp.arange(NX)[None, :]
    over = jnp.sum((apart & (counts > CAP)).astype(jnp.int32))

    zs = jnp.arange(NZ, dtype=jnp.int32)[None, :, None]
    us = jnp.arange(KC, dtype=jnp.int32)[None, None, :]
    own_table = lax.dynamic_index_in_dim(table, x, 1, False)
    own_place = lax.dynamic_index_in_dim(place, x, 1, False)
    own_within = lax.dynamic_index_in_dim(within, x, 1, False)
    own_counts = lax.dynamic_index_in_dim(counts, x, 1, False)
    codes = (zs * BR + own_within[:, :, None]) * KC + us
    sends = compact(own_table, own_place, codes.reshape(NX, FULL), FULL)
    send_counts = jnp.where(jnp.arange(NX) == x, 0, own_counts)

    my_refs = lax.dynamic_index_in_dim(refs, x, 0, False)
    my_match = lax.dynamic_slice_in_dim(match, x * BR, BR, 0)
    my_place = lax.dynamic_index_in_dim(place, x, 0, False)
    my_place = my_place.reshape(NX, NZ, KC).transpose(1, 0, 2).reshape(NZ * NX, KC)
    my_owner = jnp.maximum(my_refs, 0) // BR
    there = lookup(my_owner, my_place)
    from_x = my_owner % NX
    us = jnp.arange(KC, dtype=jnp.int32)[None, :]
    at_home = ((my_owner // NX * BR + my_refs % BR) * KC)[:, None] + us
    away = from_x != x
    source = jnp.where(away[:, None], from_x[:, None] * 128 + there, at_home)
    slot = jnp.arange(SLOTS, dtype=jnp.int32)
    left_y = (y - slot // (KC * NCORE)) % NY
    left_core = (slot // KC + core) % NCORE
    rows = jnp.arange(BR, dtype=jnp.int32)[:, None]
    left = ((left_core * NY + left_y)[None, :] * BR + rows) * KC + (slot % KC)[None, :]
    wanted = jnp.any(my_match, axis=-1)
    aim = rows[:, :, None] * KC + my_match[..., 1].astype(jnp.int32)
    code = left[:, :, None] + 128 * aim + 1024 * source.reshape(BR, SLOTS, KC)
    wanted = wanted & jnp.stack([~away, away]).reshape(2, BR, SLOTS, 1)
    wanted = wanted.reshape(2, ITEMS)
    items = compact(wanted, places_of(wanted), code.reshape(1, ITEMS), ITEMS)
    totals = jnp.sum(wanted.astype(jnp.int32), axis=-1)
    return sends.reshape(-1), send_counts, items, totals, over, targets


def shards(pattern, matrix, atom_set, atom_slab, atom_offset):
    z, x = lax.axis_index("z"), lax.axis_index("x")
    y, core = lax.axis_index("y"), lax.axis_index("core")
    row = z * NX + x
    col = y * NCORE + core
    held = lax.all_gather(matrix, "z", axis=0, tiled=True)
    held = held.reshape(NZ * BR * KC, BS, BS)

    sends, send_counts, items, totals, over, plane_targets = plan(pattern, z, x, y, core)
    targets = lax.dynamic_slice_in_dim(plane_targets, x * BR, BR, 0)

    own_ids = row * BR + jnp.arange(BR, dtype=jnp.int32)
    on_diag = targets == own_ids[:, None]
    keep = on_diag[:, :, None, None] & jnp.eye(BS, dtype=bool)
    own_diag = jnp.sum(jnp.where(keep, matrix.astype(jnp.float32), 0.0), axis=(1, 2))
    sets = BS // ORB
    gather_sets = (
        jnp.arange(BS)[:, None] // ORB == jnp.arange(sets)[None, :]
    ).astype(jnp.float32)
    set_part = jnp.dot(own_diag, gather_sets, precision=lax.Precision.HIGHEST)
    packed = jnp.concatenate([set_part.reshape(-1), over.astype(jnp.float32)[None]])
    packed = jnp.sum(everyone(packed[None], COL), axis=0)[0]
    blocks, packed = lax.optimization_barrier((matrix, packed))
    lefts = jnp.concatenate([blocks] + [shift(blocks, "y", d) for d in range(1, NY)])
    lefts = lefts.reshape(NY * BR * KC, BS, BS)
    lefts = jnp.concatenate([lefts, shift(lefts, "core", 1)])
    set_charge = packed[: BR * sets]

    atoms_here = atom_set.shape[0]
    find = (
        atom_set[:, None] - row * atoms_here
        == jnp.arange(atoms_here, dtype=jnp.int32)[None, :]
    ).astype(jnp.float32)
    charge = jnp.dot(find, set_charge, precision=lax.Precision.HIGHEST)
    start_x = atom_slab.astype(jnp.float32) * PLANES + atom_offset[0]
    flag = jnp.broadcast_to(packed[BR * sets], charge.shape)
    packed = jnp.stack([charge, start_x, atom_offset[1], atom_offset[2], flag])
    packed = everyone(packed, ROW)
    over = jnp.sum(packed[:, 4, 0])
    trace = jnp.sum(packed[:, 0])
    weight = jax.nn.sigmoid(sharpness * (half_fill - trace / (NB * BS)))
    scale = (2.0 * weight).reshape(1)
    packed = jnp.concatenate([packed[-2:], packed, packed[:2]])
    near = lax.dynamic_slice_in_dim(packed, row, 5, 0)[:, :4]
    near = near.transpose(1, 0, 2).reshape(4, 5 * atoms_here)

    x_cells = (row * PLANES + jnp.arange(PLANES, dtype=jnp.int32)).astype(jnp.float32)
    y_cells = (col * YC + jnp.arange(YC, dtype=jnp.int32)).astype(jnp.float32)
    z_cells = jnp.arange(GZ, dtype=jnp.int32).astype(jnp.float32)
    density = collocate(
        near, x_cells, y_cells, z_cells, PLANES * NZ * NX, YC * NY * NCORE, GZ
    )

    mine = matrix.reshape(BR * KC, BS, BS)
    sends, lefts, density = lax.optimization_barrier((sends, lefts, density))
    outgoing = select(sends, send_counts, held, 0)
    first = exchange(outgoing, "x")
    begun = home_products(items[0], totals[:1], lefts, held)

    def finish(rights):
        rights = rights.reshape(-1, BS, BS)
        return away_products(items[1], totals[1:], scale, lefts, rights, begun, mine)

    def one_round(first):
        return finish(first)

    def two_rounds(first):
        rounds = [first]
        for base in range(CAP, FULL, CAP):
            rounds.append(exchange(select(sends, send_counts, held, base), "x"))
        return finish(jnp.concatenate(rounds, axis=1))

    purified = lax.cond(over > 0, two_rounds, one_round, first)
    return purified.reshape(matrix.shape), density


def solution(mesh):
    fine = Mesh(mesh.devices.reshape(NZ, NX, NY, NCORE), (*ROW, *COL))
    placed = (P(), P(ROW, COL, None, None), P(ROW), P(ROW), P(None, ROW))
    return jax.shard_map(
        shards,
        mesh=fine,
        in_specs=placed,
        out_specs=(P(ROW, COL, None, None), P(ROW, COL, None)),
        check_vma=False,
    )
```

```python
import functools

import jax
import jax.numpy as jnp
from jax import lax
from jax.experimental import pallas as pl
from jax.experimental.pallas import tpu as pltpu
from jax.sharding import Mesh, PartitionSpec as P

ORB = 8
PLANES = 4
YC = 80
GZ = 640
NZ, NX, NY, NCORE = 16, 4, 4, 2
BR, KC, SLOTS, BS, NB = 4, 2, 16, 128, 256
CAP = 12
FULL = NZ * KC
ITEMS = BR * SLOTS * KC
GROUP = 4
SUMS = BR * KC + 1
ROW = ("z", "x")
COL = ("y", "core")

sharpness = 64.0
half_fill = 0.5


def exchange(value, axis):
    return lax.all_to_all(value, axis, split_axis=0, concat_axis=0, tiled=True)


def everyone(value, axis):
    count = lax.axis_size(axis)
    spread = jnp.broadcast_to(value[None], (count, *value.shape))
    return exchange(spread, axis)


def window(delta, length):
    folded = jnp.mod(delta + 0.5 * length, length) - 0.5 * length
    inside = jnp.maximum(1.0 - folded / PLANES * (folded / PLANES), 0.0)
    return inside * inside


def collocate(near, x_cells, y_cells, z_cells, length_x, length_y, length_z):
    along_x = window(x_cells[None, :] - near[1][:, None], length_x)
    along_y = window(y_cells[None, :] - near[2][:, None], length_y)
    along_z = window(z_cells[None, :] - near[3][:, None], length_z)
    plane = near[0][:, None, None] * along_x[:, :, None] * along_y[:, None, :]
    plane = plane.reshape(near.shape[1], x_cells.shape[0] * y_cells.shape[0])
    dense = jnp.dot(plane.T, along_z, precision=lax.Precision.HIGHEST)
    return dense.reshape(x_cells.shape[0], y_cells.shape[0], z_cells.shape[0])


SMEM = pl.BlockSpec(memory_space=pltpu.SMEM)
ANYWHERE = pl.BlockSpec(memory_space=pl.ANY)
VMEM = pl.BlockSpec(memory_space=pltpu.VMEM)


def select_kernel(base, codes, counts, held, out, sems):
    def copy(d, j):
        return pltpu.make_async_copy(
            held.at[codes[d * FULL + base + j]], out.at[d, j], sems.at[d, j]
        )

    fills = [jnp.clip(counts[d] - base, 0, CAP) for d in range(NX)]
    for d in range(NX):
        lax.fori_loop(0, fills[d], lambda j, _, d=d: copy(d, j).start(), None)
    for d in range(NX):
        lax.fori_loop(0, fills[d], lambda j, _, d=d: copy(d, j).wait(), None)


def select(codes, counts, held, base):
    return pl.pallas_call(
        functools.partial(select_kernel, base),
        out_shape=jax.ShapeDtypeStruct((NX, CAP, BS, BS), jnp.bfloat16),
        in_specs=[SMEM, SMEM, ANYWHERE],
        out_specs=VMEM,
        scratch_shapes=[pltpu.SemaphoreType.DMA((NX, CAP))],
        name="select",
    )(codes, counts, held)


def run_items(items, total, lefts, rights, stride, sums):
    def multiply(q, _):
        codes = [items[q * GROUP + k] for k in range(GROUP)]
        terms = [
            jnp.dot(
                lefts[code & 127],
                rights[((code >> 10) & 127) + (code >> 17) * stride],
                preferred_element_type=jnp.float32,
            )
            for code in codes
        ]
        for k, (code, term) in enumerate(zip(codes, terms)):
            target = (code >> 7) & 7
            sums[jnp.where(q * GROUP + k < total, target, BR * KC)] += term

    lax.fori_loop(0, lax.div(total + GROUP - 1, GROUP), multiply, None)


def home_kernel(items, count, lefts, held, sums):
    sums[...] = jnp.zeros_like(sums)
    run_items(items, count[0], lefts, held, 0, sums)


def away_kernel(items, count, scale, lefts, rights, begun, mine, out, sums):
    sums[...] = begun[...]
    run_items(items, count[0], lefts, rights, rights.shape[0] // NX, sums)
    twice = scale[0]
    for o in range(BR * KC):
        value = sums[o]
        out[o] = value + twice * (mine[o].astype(jnp.float32) - value)


def items_call(kernel, name, in_specs, size, scratch):
    return pl.pallas_call(
        kernel,
        out_shape=jax.ShapeDtypeStruct((size, BS, BS), jnp.float32),
        in_specs=in_specs,
        out_specs=VMEM,
        scratch_shapes=scratch,
        compiler_params=pltpu.CompilerParams(vmem_limit_bytes=24 * 1024 * 1024),
        cost_estimate=pl.CostEstimate(
            flops=2 * 16 * BS**3, bytes_accessed=6 << 20, transcendentals=0
        ),
        name=name,
    )


def home_products(items, count, lefts, held):
    call = items_call(home_kernel, "home", [SMEM] * 2 + [VMEM] * 2, SUMS, [])
    return call(items, count, lefts, held)


def away_products(items, count, scale, lefts, rights, begun, mine):
    specs = [SMEM] * 3 + [VMEM] * 4
    sums = pltpu.VMEM((SUMS, BS, BS), jnp.float32)
    call = items_call(away_kernel, "away", specs, BR * KC, [sums])
    return call(items, count, scale, lefts, rights, begun, mine)


def compact(wanted, places, codes, slots):
    hit = wanted[..., None, :] & (places[..., None, :] == jnp.arange(slots)[:, None])
    return jnp.sum(jnp.where(hit, codes[..., None, :], 0), axis=-1)


def places_of(wanted):
    size = wanted.shape[-1]
    before = jnp.arange(size)[None, :] < jnp.arange(size)[:, None]
    return jnp.sum((wanted[..., None, :] & before).astype(jnp.int32), axis=-1)


def lookup(index, table):
    chosen = index[:, None] == jnp.arange(table.shape[0], dtype=jnp.int32)[None, :]
    found = jnp.dot(
        chosen.astype(jnp.bfloat16),
        table.astype(jnp.bfloat16),
        preferred_element_type=jnp.float32,
    )
    return found.astype(jnp.int32)


def plan(pattern, z, x, y, core):
    col = y * NCORE + core
    plane = lax.dynamic_slice_in_dim(pattern, z * NX * BR, NX * BR, 0)
    group = lax.dynamic_slice_in_dim(pattern, col * KC, KC, 1)
    targets = lax.dynamic_slice_in_dim(plane, col * KC, KC, 1)
    named = lookup(plane.reshape(-1), group).reshape(NX * BR, SLOTS, KC)
    match = (
        (named[..., None] == targets[:, None, None, :])
        & (plane >= 0)[:, :, None, None]
        & (targets >= 0)[:, None, None, :]
    )
    need = jnp.any(match, axis=-1).reshape(NX, BR * SLOTS, KC)
    refs = plane.reshape(NX, BR * SLOTS)
    owner = jnp.where(refs >= 0, refs // BR, -1)
    hit = owner[:, :, None] == jnp.arange(NZ * NX, dtype=jnp.int32)
    table = jnp.stack(
        [jnp.any(hit & need[:, :, u : u + 1], axis=1) for u in range(KC)], axis=-1
    )
    within = jnp.max(jnp.where(hit, (refs % BR)[:, :, None], 0), axis=1)
    table = table.reshape(NX, NZ, NX, KC).transpose(0, 2, 1, 3).reshape(NX, NX, FULL)
    within = within.reshape(NX, NZ, NX).transpose(0, 2, 1)
    place = places_of(table)
    counts = jnp.sum(table.astype(jnp.int32), axis=-1)
    apart = jnp.arange(NX)[:, None] != jnp.arange(NX)[None, :]
    over = jnp.sum((apart & (counts > CAP)).astype(jnp.int32))

    zs = jnp.arange(NZ, dtype=jnp.int32)[None, :, None]
    us = jnp.arange(KC, dtype=jnp.int32)[None, None, :]
    own_table = lax.dynamic_index_in_dim(table, x, 1, False)
    own_place = lax.dynamic_index_in_dim(place, x, 1, False)
    own_within = lax.dynamic_index_in_dim(within, x, 1, False)
    own_counts = lax.dynamic_index_in_dim(counts, x, 1, False)
    codes = (zs * BR + own_within[:, :, None]) * KC + us
    sends = compact(own_table, own_place, codes.reshape(NX, FULL), FULL)
    send_counts = jnp.where(jnp.arange(NX) == x, 0, own_counts)

    my_refs = lax.dynamic_index_in_dim(refs, x, 0, False)
    my_match = lax.dynamic_slice_in_dim(match, x * BR, BR, 0)
    my_place = lax.dynamic_index_in_dim(place, x, 0, False)
    my_place = my_place.reshape(NX, NZ, KC).transpose(1, 0, 2).reshape(NZ * NX, KC)
    my_owner = jnp.maximum(my_refs, 0) // BR
    there = lookup(my_owner, my_place)
    from_x = my_owner % NX
    us = jnp.arange(KC, dtype=jnp.int32)[None, :]
    at_home = ((my_owner // NX * BR + my_refs % BR) * KC)[:, None] + us
    away = from_x != x
    source = jnp.where(away[:, None], from_x[:, None] * 128 + there, at_home)
    slot = jnp.arange(SLOTS, dtype=jnp.int32)
    rows = jnp.arange(BR, dtype=jnp.int32)[:, None]
    left = ((slot // KC)[None, :] * BR + rows) * KC + (slot % KC)[None, :]
    wanted = jnp.any(my_match, axis=-1)
    aim = rows[:, :, None] * KC + my_match[..., 1].astype(jnp.int32)
    code = left[:, :, None] + 128 * aim + 1024 * source.reshape(BR, SLOTS, KC)
    wanted = wanted & jnp.stack([~away, away]).reshape(2, BR, SLOTS, 1)
    wanted = wanted.reshape(2, ITEMS)
    items = compact(wanted, places_of(wanted), code.reshape(1, ITEMS), ITEMS)
    totals = jnp.sum(wanted.astype(jnp.int32), axis=-1)
    return sends.reshape(-1), send_counts, items, totals, over, targets


def shards(pattern, matrix, atom_set, atom_slab, atom_offset):
    z, x = lax.axis_index("z"), lax.axis_index("x")
    y, core = lax.axis_index("y"), lax.axis_index("core")
    row = z * NX + x
    col = y * NCORE + core
    held = lax.all_gather(matrix, "z", axis=0, tiled=True)
    held = held.reshape(NZ * BR * KC, BS, BS)

    sends, send_counts, items, totals, over, plane_targets = plan(pattern, z, x, y, core)
    targets = lax.dynamic_slice_in_dim(plane_targets, x * BR, BR, 0)

    own_ids = row * BR + jnp.arange(BR, dtype=jnp.int32)
    on_diag = targets == own_ids[:, None]
    keep = on_diag[:, :, None, None] & jnp.eye(BS, dtype=bool)
    own_diag = jnp.sum(jnp.where(keep, matrix.astype(jnp.float32), 0.0), axis=(1, 2))
    sets = BS // ORB
    gather_sets = (
        jnp.arange(BS)[:, None] // ORB == jnp.arange(sets)[None, :]
    ).astype(jnp.float32)
    set_part = jnp.dot(own_diag, gather_sets, precision=lax.Precision.HIGHEST)
    packed = jnp.concatenate([set_part.reshape(-1), over.astype(jnp.float32)[None]])
    packed = jnp.sum(everyone(packed[None], COL), axis=0)[0]
    blocks, packed = lax.optimization_barrier((matrix, packed))
    lefts = everyone(blocks, COL).reshape(SLOTS * BR, BS, BS)
    set_charge = packed[: BR * sets]

    atoms_here = atom_set.shape[0]
    find = (
        atom_set[:, None] - row * atoms_here
        == jnp.arange(atoms_here, dtype=jnp.int32)[None, :]
    ).astype(jnp.float32)
    charge = jnp.dot(find, set_charge, precision=lax.Precision.HIGHEST)
    start_x = atom_slab.astype(jnp.float32) * PLANES + atom_offset[0]
    flag = jnp.broadcast_to(packed[BR * sets], charge.shape)
    packed = jnp.stack([charge, start_x, atom_offset[1], atom_offset[2], flag])
    packed = lax.all_gather(everyone(packed, "x"), "z", axis=0, tiled=False)
    packed = packed.reshape(NZ * NX, 5, atoms_here)
    over = jnp.sum(packed[:, 4, 0])
    trace = jnp.sum(packed[:, 0])
    weight = jax.nn.sigmoid(sharpness * (half_fill - trace / (NB * BS)))
    scale = (2.0 * weight).reshape(1)
    packed = jnp.concatenate([packed[-2:], packed, packed[:2]])
    near = lax.dynamic_slice_in_dim(packed, row, 5, 0)[:, :4]
    near = near.transpose(1, 0, 2).reshape(4, 5 * atoms_here)

    x_cells = (row * PLANES + jnp.arange(PLANES, dtype=jnp.int32)).astype(jnp.float32)
    y_cells = (col * YC + jnp.arange(YC, dtype=jnp.int32)).astype(jnp.float32)
    z_cells = jnp.arange(GZ, dtype=jnp.int32).astype(jnp.float32)
    density = collocate(
        near, x_cells, y_cells, z_cells, PLANES * NZ * NX, YC * NY * NCORE, GZ
    )

    mine = matrix.reshape(BR * KC, BS, BS)
    sends, lefts, density = lax.optimization_barrier((sends, lefts, density))
    outgoing = select(sends, send_counts, held, 0)
    first = exchange(outgoing, "x")
    begun = home_products(items[0], totals[:1], lefts, held)

    def finish(rights):
        rights = rights.reshape(-1, BS, BS)
        return away_products(items[1], totals[1:], scale, lefts, rights, begun, mine)

    def one_round(first):
        return finish(first)

    def two_rounds(first):
        rounds = [first]
        for base in range(CAP, FULL, CAP):
            rounds.append(exchange(select(sends, send_counts, held, base), "x"))
        return finish(jnp.concatenate(rounds, axis=1))

    purified = lax.cond(over > 0, two_rounds, one_round, first)
    return purified.reshape(matrix.shape), density


def solution(mesh):
    fine = Mesh(mesh.devices.reshape(NZ, NX, NY, NCORE), (*ROW, *COL))
    placed = (P(), P(ROW, COL, None, None), P(ROW), P(ROW), P(None, ROW))
    return jax.shard_map(
        shards,
        mesh=fine,
        in_specs=placed,
        out_specs=(P(ROW, COL, None, None), P(ROW, COL, None)),
        check_vma=False,
    )
```

```python
import functools

import jax
import jax.numpy as jnp
from jax import lax
from jax.experimental import pallas as pl
from jax.experimental.pallas import tpu as pltpu
from jax.sharding import Mesh, PartitionSpec as P

ORB = 8
PLANES = 4
YC = 80
GZ = 640
NZ, NX, NY, NCORE = 16, 4, 4, 2
BR, KC, SLOTS, BS, NB = 4, 2, 16, 128, 256
CAP = 12
FULL = NZ * KC
ITEMS = BR * SLOTS * KC
GROUP = 4
SUMS = BR * KC + 1
ROW = ("z", "x")
COL = ("y", "core")

sharpness = 64.0
half_fill = 0.5


def exchange(value, axis):
    return lax.all_to_all(value, axis, split_axis=0, concat_axis=0, tiled=True)


def everyone(value, axis):
    count = lax.axis_size(axis)
    spread = jnp.broadcast_to(value[None], (count, *value.shape))
    return exchange(spread, axis)


def window(delta, length):
    folded = jnp.mod(delta + 0.5 * length, length) - 0.5 * length
    inside = jnp.maximum(1.0 - folded / PLANES * (folded / PLANES), 0.0)
    return inside * inside


def collocate(near, x_cells, y_cells, z_cells, length_x, length_y, length_z):
    along_x = window(x_cells[None, :] - near[1][:, None], length_x)
    along_y = window(y_cells[None, :] - near[2][:, None], length_y)
    along_z = window(z_cells[None, :] - near[3][:, None], length_z)
    plane = near[0][:, None, None] * along_x[:, :, None] * along_y[:, None, :]
    plane = plane.reshape(near.shape[1], x_cells.shape[0] * y_cells.shape[0])
    dense = jnp.dot(plane.T, along_z, precision=lax.Precision.HIGHEST)
    return dense.reshape(x_cells.shape[0], y_cells.shape[0], z_cells.shape[0])


SMEM = pl.BlockSpec(memory_space=pltpu.SMEM)
ANYWHERE = pl.BlockSpec(memory_space=pl.ANY)
VMEM = pl.BlockSpec(memory_space=pltpu.VMEM)


def select_kernel(base, codes, held, out, stage, in_sems, out_sems):
    def fetch(d, j):
        return pltpu.make_async_copy(
            held.at[codes[d * FULL + base + j]], stage.at[d, j], in_sems.at[d, j]
        )

    def store(d, j):
        return pltpu.make_async_copy(stage.at[d, j], out.at[d, j], out_sems.at[d, j])

    def pass_on(d, j):
        fetch(d, j).wait()
        store(d, j).start()

    fills = [jnp.clip(codes[NX * FULL + d] - base, 0, CAP) for d in range(NX)]
    for d in range(NX):
        lax.fori_loop(0, fills[d], lambda j, _, d=d: fetch(d, j).start(), None)
    for d in range(NX):
        lax.fori_loop(0, fills[d], lambda j, _, d=d: pass_on(d, j), None)
    for d in range(NX):
        lax.fori_loop(0, fills[d], lambda j, _, d=d: store(d, j).wait(), None)


def select(codes, held, base):
    return pl.pallas_call(
        functools.partial(select_kernel, base),
        out_shape=jax.ShapeDtypeStruct((NX, CAP, BS, BS), jnp.bfloat16),
        in_specs=[SMEM, ANYWHERE],
        out_specs=ANYWHERE,
        scratch_shapes=[
            pltpu.VMEM((NX, CAP, BS, BS), jnp.bfloat16),
            pltpu.SemaphoreType.DMA((NX, CAP)),
            pltpu.SemaphoreType.DMA((NX, CAP)),
        ],
        name="select",
    )(codes, held)


def run_items(items, lefts, rights, stride, sums):
    total = items[ITEMS]

    def multiply(q, _):
        codes = [items[q * GROUP + k] for k in range(GROUP)]
        terms = [
            jnp.dot(
                lefts[code & 127],
                rights[((code >> 10) & 127) + (code >> 17) * stride],
                preferred_element_type=jnp.float32,
            )
            for code in codes
        ]
        for k, (code, term) in enumerate(zip(codes, terms)):
            target = (code >> 7) & 7
            sums[jnp.where(q * GROUP + k < total, target, BR * KC)] += term

    lax.fori_loop(0, lax.div(total + GROUP - 1, GROUP), multiply, None)


def home_kernel(items, lefts, held, sums):
    sums[...] = jnp.zeros_like(sums)
    run_items(items, lefts, held, 0, sums)


def away_kernel(items, scale, lefts, rights, begun, mine, out, sums, sems):
    sums[...] = begun[...]
    run_items(items, lefts, rights, rights.shape[0] // NX, sums)
    twice = scale[0]

    def store(o):
        return pltpu.make_async_copy(sums.at[o], out.at[o], sems.at[o])

    for o in range(BR * KC):
        value = sums[o]
        sums[o] = value + twice * (mine[o].astype(jnp.float32) - value)
        store(o).start()
    for o in range(BR * KC):
        store(o).wait()


def items_call(kernel, name, in_specs, out_spec, size, scratch):
    return pl.pallas_call(
        kernel,
        out_shape=jax.ShapeDtypeStruct((size, BS, BS), jnp.float32),
        in_specs=in_specs,
        out_specs=out_spec,
        scratch_shapes=scratch,
        compiler_params=pltpu.CompilerParams(vmem_limit_bytes=24 * 1024 * 1024),
        cost_estimate=pl.CostEstimate(
            flops=2 * 16 * BS**3, bytes_accessed=6 << 20, transcendentals=0
        ),
        name=name,
    )


def home_products(items, lefts, held):
    call = items_call(home_kernel, "home", [SMEM] + [VMEM] * 2, VMEM, SUMS, [])
    return call(items, lefts, held)


def away_products(items, scale, lefts, rights, begun, mine):
    scratch = [
        pltpu.VMEM((SUMS, BS, BS), jnp.float32),
        pltpu.SemaphoreType.DMA((BR * KC,)),
    ]
    specs = [SMEM] * 2 + [VMEM] * 4
    out_spec = pl.BlockSpec(memory_space=pltpu.HBM)
    call = items_call(away_kernel, "away", specs, out_spec, BR * KC, scratch)
    return call(items, scale, lefts, rights, begun, mine)


def compact(wanted, places, codes, slots):
    hit = wanted[..., None, :] & (places[..., None, :] == jnp.arange(slots)[:, None])
    return jnp.sum(jnp.where(hit, codes[..., None, :], 0), axis=-1)


def places_of(wanted):
    size = wanted.shape[-1]
    before = jnp.arange(size)[None, :] < jnp.arange(size)[:, None]
    return jnp.sum((wanted[..., None, :] & before).astype(jnp.int32), axis=-1)


def lookup(index, table):
    chosen = index[:, None] == jnp.arange(table.shape[0], dtype=jnp.int32)[None, :]
    found = jnp.dot(
        chosen.astype(jnp.bfloat16),
        table.astype(jnp.bfloat16),
        preferred_element_type=jnp.float32,
    )
    return found.astype(jnp.int32)


def plan(pattern, z, x, y, core):
    col = y * NCORE + core
    plane = lax.dynamic_slice_in_dim(pattern, z * NX * BR, NX * BR, 0)
    group = lax.dynamic_slice_in_dim(pattern, col * KC, KC, 1)
    targets = lax.dynamic_slice_in_dim(plane, col * KC, KC, 1)
    named = lookup(plane.reshape(-1), group).reshape(NX * BR, SLOTS, KC)
    match = (
        (named[..., None] == targets[:, None, None, :])
        & (plane >= 0)[:, :, None, None]
        & (targets >= 0)[:, None, None, :]
    )
    need = jnp.any(match, axis=-1).reshape(NX, BR * SLOTS, KC)
    refs = plane.reshape(NX, BR * SLOTS)
    owner = jnp.where(refs >= 0, refs // BR, -1)
    hit = owner[:, :, None] == jnp.arange(NZ * NX, dtype=jnp.int32)
    table = jnp.stack(
        [jnp.any(hit & need[:, :, u : u + 1], axis=1) for u in range(KC)], axis=-1
    )
    within = jnp.max(jnp.where(hit, (refs % BR)[:, :, None], 0), axis=1)
    table = table.reshape(NX, NZ, NX, KC).transpose(0, 2, 1, 3).reshape(NX, NX, FULL)
    within = within.reshape(NX, NZ, NX).transpose(0, 2, 1)
    place = places_of(table)
    counts = jnp.sum(table.astype(jnp.int32), axis=-1)
    apart = jnp.arange(NX)[:, None] != jnp.arange(NX)[None, :]
    over = jnp.sum((apart & (counts > CAP)).astype(jnp.int32))

    zs = jnp.arange(NZ, dtype=jnp.int32)[None, :, None]
    us = jnp.arange(KC, dtype=jnp.int32)[None, None, :]
    own_table = lax.dynamic_index_in_dim(table, x, 1, False)
    own_place = lax.dynamic_index_in_dim(place, x, 1, False)
    own_within = lax.dynamic_index_in_dim(within, x, 1, False)
    own_counts = lax.dynamic_index_in_dim(counts, x, 1, False)
    codes = (zs * BR + own_within[:, :, None]) * KC + us
    sends = compact(own_table, own_place, codes.reshape(NX, FULL), FULL)
    send_counts = jnp.where(jnp.arange(NX) == x, 0, own_counts)

    my_refs = lax.dynamic_index_in_dim(refs, x, 0, False)
    my_match = lax.dynamic_slice_in_dim(match, x * BR, BR, 0)
    my_place = lax.dynamic_index_in_dim(place, x, 0, False)
    my_place = my_place.reshape(NX, NZ, KC).transpose(1, 0, 2).reshape(NZ * NX, KC)
    my_owner = jnp.maximum(my_refs, 0) // BR
    there = lookup(my_owner, my_place)
    from_x = my_owner % NX
    us = jnp.arange(KC, dtype=jnp.int32)[None, :]
    at_home = ((my_owner // NX * BR + my_refs % BR) * KC)[:, None] + us
    away = from_x != x
    source = jnp.where(away[:, None], from_x[:, None] * 128 + there, at_home)
    slot = jnp.arange(SLOTS, dtype=jnp.int32)
    rows = jnp.arange(BR, dtype=jnp.int32)[:, None]
    left = ((slot // KC)[None, :] * BR + rows) * KC + (slot % KC)[None, :]
    wanted = jnp.any(my_match, axis=-1)
    aim = rows[:, :, None] * KC + my_match[..., 1].astype(jnp.int32)
    code = left[:, :, None] + 128 * aim + 1024 * source.reshape(BR, SLOTS, KC)
    wanted = wanted & jnp.stack([~away, away]).reshape(2, BR, SLOTS, 1)
    wanted = wanted.reshape(2, ITEMS)
    items = compact(wanted, places_of(wanted), code.reshape(1, ITEMS), ITEMS)
    totals = jnp.sum(wanted.astype(jnp.int32), axis=-1)
    sends = jnp.concatenate([sends.reshape(-1), send_counts])
    items = jnp.concatenate([items, totals[:, None]], axis=1)
    return sends, items, over, targets


def shards(pattern, matrix, atom_set, atom_slab, atom_offset):
    z, x = lax.axis_index("z"), lax.axis_index("x")
    y, core = lax.axis_index("y"), lax.axis_index("core")
    row = z * NX + x
    col = y * NCORE + core
    held = lax.all_gather(matrix, "z", axis=0, tiled=True)
    held = held.reshape(NZ * BR * KC, BS, BS)

    sends, items, over, plane_targets = plan(pattern, z, x, y, core)
    targets = lax.dynamic_slice_in_dim(plane_targets, x * BR, BR, 0)

    own_ids = row * BR + jnp.arange(BR, dtype=jnp.int32)
    on_diag = targets == own_ids[:, None]
    keep = on_diag[:, :, None, None] & jnp.eye(BS, dtype=bool)
    own_diag = jnp.sum(jnp.where(keep, matrix.astype(jnp.float32), 0.0), axis=(1, 2))
    sets = BS // ORB
    gather_sets = (
        jnp.arange(BS)[:, None] // ORB == jnp.arange(sets)[None, :]
    ).astype(jnp.float32)
    set_part = jnp.dot(own_diag, gather_sets, precision=lax.Precision.HIGHEST)
    packed = jnp.concatenate([set_part.reshape(-1), over.astype(jnp.float32)[None]])
    packed = jnp.sum(everyone(packed[None], COL), axis=0)[0]
    blocks, packed = lax.optimization_barrier((matrix, packed))
    lefts = everyone(blocks, COL).reshape(SLOTS * BR, BS, BS)
    set_charge = packed[: BR * sets]

    atoms_here = atom_set.shape[0]
    find = (
        atom_set[:, None] - row * atoms_here
        == jnp.arange(atoms_here, dtype=jnp.int32)[None, :]
    ).astype(jnp.float32)
    charge = jnp.dot(find, set_charge, precision=lax.Precision.HIGHEST)
    start_x = atom_slab.astype(jnp.float32) * PLANES + atom_offset[0]
    flag = jnp.broadcast_to(packed[BR * sets], charge.shape)
    packed = jnp.stack([charge, start_x, atom_offset[1], atom_offset[2], flag])
    packed = lax.all_gather(everyone(packed, "x"), "z", axis=0, tiled=False)
    packed = packed.reshape(NZ * NX, 5, atoms_here)
    over = jnp.sum(packed[:, 4, 0])
    trace = jnp.sum(packed[:, 0])
    weight = jax.nn.sigmoid(sharpness * (half_fill - trace / (NB * BS)))
    scale = (2.0 * weight).reshape(1)
    packed = jnp.concatenate([packed[-2:], packed, packed[:2]])
    near = lax.dynamic_slice_in_dim(packed, row, 5, 0)[:, :4]
    near = near.transpose(1, 0, 2).reshape(4, 5 * atoms_here)

    x_cells = (row * PLANES + jnp.arange(PLANES, dtype=jnp.int32)).astype(jnp.float32)
    y_cells = (col * YC + jnp.arange(YC, dtype=jnp.int32)).astype(jnp.float32)
    z_cells = jnp.arange(GZ, dtype=jnp.int32).astype(jnp.float32)
    density = collocate(
        near, x_cells, y_cells, z_cells, PLANES * NZ * NX, YC * NY * NCORE, GZ
    )

    mine = matrix.reshape(BR * KC, BS, BS)
    sends, lefts, density = lax.optimization_barrier((sends, lefts, density))
    outgoing = select(sends, held, 0)
    first = exchange(outgoing, "x")
    begun = home_products(items[0], lefts, held)

    def finish(rights):
        rights = rights.reshape(-1, BS, BS)
        return away_products(items[1], scale, lefts, rights, begun, mine)

    def one_round(first):
        return finish(first)

    def two_rounds(first):
        rounds = [first]
        for base in range(CAP, FULL, CAP):
            rounds.append(exchange(select(sends, held, base), "x"))
        return finish(jnp.concatenate(rounds, axis=1))

    purified = lax.cond(over > 0, two_rounds, one_round, first)
    return purified.reshape(matrix.shape), density


def solution(mesh):
    fine = Mesh(mesh.devices.reshape(NZ, NX, NY, NCORE), (*ROW, *COL))
    placed = (P(), P(ROW, COL, None, None), P(ROW), P(ROW), P(None, ROW))
    return jax.shard_map(
        shards,
        mesh=fine,
        in_specs=placed,
        out_specs=(P(ROW, COL, None, None), P(ROW, COL, None)),
        check_vma=False,
    )
```

```python
import jax
import jax.numpy as jnp
from jax import lax
from jax.experimental import pallas as pl
from jax.experimental.pallas import tpu as pltpu
from jax.sharding import Mesh, PartitionSpec as P

ORB = 8
PLANES = 4
YC = 80
GZ = 640
NZ, NX, NY, NCORE = 16, 4, 4, 2
BR, KC, SLOTS, BS, NB = 4, 2, 16, 128, 256
CAPS = (8, 9, 10, 11, 12, 16, 24, 32)
FULL = NZ * KC
ITEMS = BR * SLOTS * KC
GROUP = 4
SUMS = BR * KC + 1
ROW = ("z", "x")
COL = ("y", "core")

sharpness = 64.0
half_fill = 0.5


def exchange(value, axis):
    return lax.all_to_all(value, axis, split_axis=0, concat_axis=0, tiled=True)


def everyone(value, axis):
    count = lax.axis_size(axis)
    spread = jnp.broadcast_to(value[None], (count, *value.shape))
    return exchange(spread, axis)


def window(delta, length):
    folded = jnp.mod(delta + 0.5 * length, length) - 0.5 * length
    inside = jnp.maximum(1.0 - folded / PLANES * (folded / PLANES), 0.0)
    return inside * inside


def collocate(near, x_cells, y_cells, z_cells, length_x, length_y, length_z):
    along_x = window(x_cells[None, :] - near[1][:, None], length_x)
    along_y = window(y_cells[None, :] - near[2][:, None], length_y)
    along_z = window(z_cells[None, :] - near[3][:, None], length_z)
    plane = near[0][:, None, None] * along_x[:, :, None] * along_y[:, None, :]
    plane = plane.reshape(near.shape[1], x_cells.shape[0] * y_cells.shape[0])
    dense = jnp.dot(plane.T, along_z, precision=lax.Precision.HIGHEST)
    return dense.reshape(x_cells.shape[0], y_cells.shape[0], z_cells.shape[0])


SMEM = pl.BlockSpec(memory_space=pltpu.SMEM)
ANYWHERE = pl.BlockSpec(memory_space=pl.ANY)
VMEM = pl.BlockSpec(memory_space=pltpu.VMEM)


def select_kernel(codes, held, out, stage, in_sems, out_sems):
    def fetch(d, j):
        return pltpu.make_async_copy(
            held.at[codes[d * FULL + j]], stage.at[d, j], in_sems.at[d, j]
        )

    def store(d, j):
        return pltpu.make_async_copy(stage.at[d, j], out.at[d, j], out_sems.at[d, j])

    def pass_on(d, j):
        fetch(d, j).wait()
        store(d, j).start()

    fills = [jnp.minimum(codes[NX * FULL + d], out.shape[1]) for d in range(NX)]
    for d in range(NX):
        lax.fori_loop(0, fills[d], lambda j, _, d=d: fetch(d, j).start(), None)
    for d in range(NX):
        lax.fori_loop(0, fills[d], lambda j, _, d=d: pass_on(d, j), None)
    for d in range(NX):
        lax.fori_loop(0, fills[d], lambda j, _, d=d: store(d, j).wait(), None)


def select(codes, held, cap):
    return pl.pallas_call(
        select_kernel,
        out_shape=jax.ShapeDtypeStruct((NX, cap, BS, BS), jnp.bfloat16),
        in_specs=[SMEM, ANYWHERE],
        out_specs=ANYWHERE,
        scratch_shapes=[
            pltpu.VMEM((NX, cap, BS, BS), jnp.bfloat16),
            pltpu.SemaphoreType.DMA((NX, cap)),
            pltpu.SemaphoreType.DMA((NX, cap)),
        ],
        name="select",
    )(codes, held)


def run_items(items, lefts, rights, stride, sums):
    total = items[ITEMS]

    def multiply(q, _):
        codes = [items[q * GROUP + k] for k in range(GROUP)]
        terms = [
            jnp.dot(
                lefts[code & 127],
                rights[((code >> 10) & 127) + (code >> 17) * stride],
                preferred_element_type=jnp.float32,
            )
            for code in codes
        ]
        for k, (code, term) in enumerate(zip(codes, terms)):
            target = (code >> 7) & 7
            sums[jnp.where(q * GROUP + k < total, target, BR * KC)] += term

    lax.fori_loop(0, lax.div(total + GROUP - 1, GROUP), multiply, None)


def home_kernel(items, lefts, held, sums):
    sums[...] = jnp.zeros_like(sums)
    run_items(items, lefts, held, 0, sums)


def away_kernel(items, scale, lefts, rights, begun, mine, out, sums, sems):
    sums[...] = begun[...]
    run_items(items, lefts, rights, rights.shape[0] // NX, sums)
    twice = scale[0]

    def store(o):
        return pltpu.make_async_copy(sums.at[o], out.at[o], sems.at[o])

    for o in range(BR * KC):
        value = sums[o]
        sums[o] = value + twice * (mine[o].astype(jnp.float32) - value)
        store(o).start()
    for o in range(BR * KC):
        store(o).wait()


def items_call(kernel, name, in_specs, out_spec, size, scratch):
    return pl.pallas_call(
        kernel,
        out_shape=jax.ShapeDtypeStruct((size, BS, BS), jnp.float32),
        in_specs=in_specs,
        out_specs=out_spec,
        scratch_shapes=scratch,
        compiler_params=pltpu.CompilerParams(vmem_limit_bytes=24 * 1024 * 1024),
        cost_estimate=pl.CostEstimate(
            flops=2 * 16 * BS**3, bytes_accessed=6 << 20, transcendentals=0
        ),
        name=name,
    )


def home_products(items, lefts, held):
    call = items_call(home_kernel, "home", [SMEM] + [VMEM] * 2, VMEM, SUMS, [])
    return call(items, lefts, held)


def away_products(items, scale, lefts, rights, begun, mine):
    scratch = [
        pltpu.VMEM((SUMS, BS, BS), jnp.float32),
        pltpu.SemaphoreType.DMA((BR * KC,)),
    ]
    specs = [SMEM] * 2 + [VMEM] * 4
    out_spec = pl.BlockSpec(memory_space=pltpu.HBM)
    call = items_call(away_kernel, "away", specs, out_spec, BR * KC, scratch)
    return call(items, scale, lefts, rights, begun, mine)


def compact(wanted, places, codes, slots):
    hit = wanted[..., None, :] & (places[..., None, :] == jnp.arange(slots)[:, None])
    return jnp.sum(jnp.where(hit, codes[..., None, :], 0), axis=-1)


def places_of(wanted):
    size = wanted.shape[-1]
    before = jnp.arange(size)[None, :] < jnp.arange(size)[:, None]
    return jnp.sum((wanted[..., None, :] & before).astype(jnp.int32), axis=-1)


def lookup(index, table):
    chosen = index[:, None] == jnp.arange(table.shape[0], dtype=jnp.int32)[None, :]
    found = jnp.dot(
        chosen.astype(jnp.bfloat16),
        table.astype(jnp.bfloat16),
        preferred_element_type=jnp.float32,
    )
    return found.astype(jnp.int32)


def plan(pattern, z, x, y, core):
    col = y * NCORE + core
    plane = lax.dynamic_slice_in_dim(pattern, z * NX * BR, NX * BR, 0)
    group = lax.dynamic_slice_in_dim(pattern, col * KC, KC, 1)
    targets = lax.dynamic_slice_in_dim(plane, col * KC, KC, 1)
    named = lookup(plane.reshape(-1), group).reshape(NX * BR, SLOTS, KC)
    match = (
        (named[..., None] == targets[:, None, None, :])
        & (plane >= 0)[:, :, None, None]
        & (targets >= 0)[:, None, None, :]
    )
    need = jnp.any(match, axis=-1).reshape(NX, BR * SLOTS, KC)
    refs = plane.reshape(NX, BR * SLOTS)
    owner = jnp.where(refs >= 0, refs // BR, -1)
    hit = owner[:, :, None] == jnp.arange(NZ * NX, dtype=jnp.int32)
    table = jnp.stack(
        [jnp.any(hit & need[:, :, u : u + 1], axis=1) for u in range(KC)], axis=-1
    )
    within = jnp.max(jnp.where(hit, (refs % BR)[:, :, None], 0), axis=1)
    table = table.reshape(NX, NZ, NX, KC).transpose(0, 2, 1, 3).reshape(NX, NX, FULL)
    within = within.reshape(NX, NZ, NX).transpose(0, 2, 1)
    place = places_of(table)
    counts = jnp.sum(table.astype(jnp.int32), axis=-1)
    apart = jnp.arange(NX)[:, None] != jnp.arange(NX)[None, :]
    most = jnp.max(jnp.where(apart, counts, 0))

    zs = jnp.arange(NZ, dtype=jnp.int32)[None, :, None]
    us = jnp.arange(KC, dtype=jnp.int32)[None, None, :]
    own_table = lax.dynamic_index_in_dim(table, x, 1, False)
    own_place = lax.dynamic_index_in_dim(place, x, 1, False)
    own_within = lax.dynamic_index_in_dim(within, x, 1, False)
    own_counts = lax.dynamic_index_in_dim(counts, x, 1, False)
    codes = (zs * BR + own_within[:, :, None]) * KC + us
    sends = compact(own_table, own_place, codes.reshape(NX, FULL), FULL)
    send_counts = jnp.where(jnp.arange(NX) == x, 0, own_counts)

    my_refs = lax.dynamic_index_in_dim(refs, x, 0, False)
    my_match = lax.dynamic_slice_in_dim(match, x * BR, BR, 0)
    my_place = lax.dynamic_index_in_dim(place, x, 0, False)
    my_place = my_place.reshape(NX, NZ, KC).transpose(1, 0, 2).reshape(NZ * NX, KC)
    my_owner = jnp.maximum(my_refs, 0) // BR
    there = lookup(my_owner, my_place)
    from_x = my_owner % NX
    us = jnp.arange(KC, dtype=jnp.int32)[None, :]
    at_home = ((my_owner // NX * BR + my_refs % BR) * KC)[:, None] + us
    away = from_x != x
    source = jnp.where(away[:, None], from_x[:, None] * 128 + there, at_home)
    slot = jnp.arange(SLOTS, dtype=jnp.int32)
    rows = jnp.arange(BR, dtype=jnp.int32)[:, None]
    left = ((slot // KC)[None, :] * BR + rows) * KC + (slot % KC)[None, :]
    wanted = jnp.any(my_match, axis=-1)
    aim = rows[:, :, None] * KC + my_match[..., 1].astype(jnp.int32)
    code = left[:, :, None] + 128 * aim + 1024 * source.reshape(BR, SLOTS, KC)
    wanted = wanted & jnp.stack([~away, away]).reshape(2, BR, SLOTS, 1)
    wanted = wanted.reshape(2, ITEMS)
    items = compact(wanted, places_of(wanted), code.reshape(1, ITEMS), ITEMS)
    totals = jnp.sum(wanted.astype(jnp.int32), axis=-1)
    sends = jnp.concatenate([sends.reshape(-1), send_counts])
    items = jnp.concatenate([items, totals[:, None]], axis=1)
    return sends, items, most, targets


def shards(pattern, matrix, atom_set, atom_slab, atom_offset):
    z, x = lax.axis_index("z"), lax.axis_index("x")
    y, core = lax.axis_index("y"), lax.axis_index("core")
    row = z * NX + x
    col = y * NCORE + core
    held = lax.all_gather(matrix, "z", axis=0, tiled=True)
    held = held.reshape(NZ * BR * KC, BS, BS)

    sends, items, most, plane_targets = plan(pattern, z, x, y, core)
    targets = lax.dynamic_slice_in_dim(plane_targets, x * BR, BR, 0)

    own_ids = row * BR + jnp.arange(BR, dtype=jnp.int32)
    on_diag = targets == own_ids[:, None]
    keep = on_diag[:, :, None, None] & jnp.eye(BS, dtype=bool)
    own_diag = jnp.sum(jnp.where(keep, matrix.astype(jnp.float32), 0.0), axis=(1, 2))
    sets = BS // ORB
    gather_sets = (
        jnp.arange(BS)[:, None] // ORB == jnp.arange(sets)[None, :]
    ).astype(jnp.float32)
    set_part = jnp.dot(own_diag, gather_sets, precision=lax.Precision.HIGHEST)
    packed = jnp.concatenate([set_part.reshape(-1), most.astype(jnp.float32)[None]])
    packed = everyone(packed[None], COL)[:, 0]
    most = jnp.max(packed[:, BR * sets])
    packed = jnp.sum(packed, axis=0)
    blocks, packed = lax.optimization_barrier((matrix, packed))
    lefts = everyone(blocks, COL).reshape(SLOTS * BR, BS, BS)
    set_charge = packed[: BR * sets]

    atoms_here = atom_set.shape[0]
    find = (
        atom_set[:, None] - row * atoms_here
        == jnp.arange(atoms_here, dtype=jnp.int32)[None, :]
    ).astype(jnp.float32)
    charge = jnp.dot(find, set_charge, precision=lax.Precision.HIGHEST)
    start_x = atom_slab.astype(jnp.float32) * PLANES + atom_offset[0]
    flag = jnp.broadcast_to(most, charge.shape)
    packed = jnp.stack([charge, start_x, atom_offset[1], atom_offset[2], flag])
    packed = lax.all_gather(everyone(packed, "x"), "z", axis=0, tiled=False)
    packed = packed.reshape(NZ * NX, 5, atoms_here)
    most = jnp.max(packed[:, 4, 0])
    trace = jnp.sum(packed[:, 0])
    weight = jax.nn.sigmoid(sharpness * (half_fill - trace / (NB * BS)))
    scale = (2.0 * weight).reshape(1)
    packed = jnp.concatenate([packed[-2:], packed, packed[:2]])
    near = lax.dynamic_slice_in_dim(packed, row, 5, 0)[:, :4]
    near = near.transpose(1, 0, 2).reshape(4, 5 * atoms_here)

    x_cells = (row * PLANES + jnp.arange(PLANES, dtype=jnp.int32)).astype(jnp.float32)
    y_cells = (col * YC + jnp.arange(YC, dtype=jnp.int32)).astype(jnp.float32)
    z_cells = jnp.arange(GZ, dtype=jnp.int32).astype(jnp.float32)
    density = collocate(
        near, x_cells, y_cells, z_cells, PLANES * NZ * NX, YC * NY * NCORE, GZ
    )

    mine = matrix.reshape(BR * KC, BS, BS)
    sends, lefts, density = lax.optimization_barrier((sends, lefts, density))

    def with_slots(cap):
        def run(sends, items, scale, lefts, held, mine):
            rights = exchange(select(sends, held, cap), "x").reshape(-1, BS, BS)
            begun = home_products(items[0], lefts, held)
            return away_products(items[1], scale, lefts, rights, begun, mine)

        return run

    size = sum((most > cap).astype(jnp.int32) for cap in CAPS[:-1])
    purified = lax.switch(
        size, [with_slots(cap) for cap in CAPS], sends, items, scale, lefts, held, mine
    )
    return purified.reshape(matrix.shape), density


def solution(mesh):
    fine = Mesh(mesh.devices.reshape(NZ, NX, NY, NCORE), (*ROW, *COL))
    placed = (P(), P(ROW, COL, None, None), P(ROW), P(ROW), P(None, ROW))
    return jax.shard_map(
        shards,
        mesh=fine,
        in_specs=placed,
        out_specs=(P(ROW, COL, None, None), P(ROW, COL, None)),
        check_vma=False,
    )
```

```python
import jax
import jax.numpy as jnp
from jax import lax
from jax.experimental import pallas as pl
from jax.experimental.pallas import tpu as pltpu
from jax.sharding import Mesh, PartitionSpec as P

ORB = 8
PLANES = 4
YC = 80
GZ = 640
NZ, NX, NY, NCORE = 16, 4, 4, 2
BR, KC, SLOTS, BS, NB = 4, 2, 16, 128, 256
CAPS = (4, 5, 6, 7, 8, 9, 10, 11, 12, 16, 24, 32)
FULL = NZ * KC
ITEMS = BR * SLOTS * KC
GROUP = 4
SUMS = BR * KC + 1
ROW = ("z", "x")
COL = ("y", "core")

sharpness = 64.0
half_fill = 0.5


def exchange(value, axis):
    return lax.all_to_all(value, axis, split_axis=0, concat_axis=0, tiled=True)


def everyone(value, axis):
    count = lax.axis_size(axis)
    spread = jnp.broadcast_to(value[None], (count, *value.shape))
    return exchange(spread, axis)


def window(delta, length):
    folded = jnp.mod(delta + 0.5 * length, length) - 0.5 * length
    inside = jnp.maximum(1.0 - folded / PLANES * (folded / PLANES), 0.0)
    return inside * inside


def collocate(near, x_cells, y_cells, z_cells, length_x, length_y, length_z):
    along_x = window(x_cells[None, :] - near[1][:, None], length_x)
    along_y = window(y_cells[None, :] - near[2][:, None], length_y)
    along_z = window(z_cells[None, :] - near[3][:, None], length_z)
    plane = near[0][:, None, None] * along_x[:, :, None] * along_y[:, None, :]
    plane = plane.reshape(near.shape[1], x_cells.shape[0] * y_cells.shape[0])
    dense = jnp.dot(plane.T, along_z, precision=lax.Precision.HIGHEST)
    return dense.reshape(x_cells.shape[0], y_cells.shape[0], z_cells.shape[0])


SMEM = pl.BlockSpec(memory_space=pltpu.SMEM)
ANYWHERE = pl.BlockSpec(memory_space=pl.ANY)
VMEM = pl.BlockSpec(memory_space=pltpu.VMEM)


def select_kernel(codes, held, out, stage, in_sems, out_sems):
    def fetch(d, j):
        return pltpu.make_async_copy(
            held.at[codes[d * FULL + j]], stage.at[d, j], in_sems.at[d, j]
        )

    def store(d, j):
        return pltpu.make_async_copy(stage.at[d, j], out.at[d, j], out_sems.at[d, j])

    def pass_on(d, j):
        fetch(d, j).wait()
        store(d, j).start()

    fills = [jnp.minimum(codes[NX * FULL + d], out.shape[1]) for d in range(NX)]
    for d in range(NX):
        lax.fori_loop(0, fills[d], lambda j, _, d=d: fetch(d, j).start(), None)
    for d in range(NX):
        lax.fori_loop(0, fills[d], lambda j, _, d=d: pass_on(d, j), None)
    for d in range(NX):
        lax.fori_loop(0, fills[d], lambda j, _, d=d: store(d, j).wait(), None)


def select(codes, held, cap):
    return pl.pallas_call(
        select_kernel,
        out_shape=jax.ShapeDtypeStruct((NX, cap, BS, BS), jnp.bfloat16),
        in_specs=[SMEM, ANYWHERE],
        out_specs=ANYWHERE,
        scratch_shapes=[
            pltpu.VMEM((NX, cap, BS, BS), jnp.bfloat16),
            pltpu.SemaphoreType.DMA((NX, cap)),
            pltpu.SemaphoreType.DMA((NX, cap)),
        ],
        name="select",
    )(codes, held)


def run_items(items, lefts, rights, stride, sums):
    total = items[ITEMS]

    def multiply(q, _):
        codes = [items[q * GROUP + k] for k in range(GROUP)]
        terms = [
            jnp.dot(
                lefts[code & 127],
                rights[((code >> 10) & 127) + (code >> 17) * stride],
                preferred_element_type=jnp.float32,
            )
            for code in codes
        ]
        for k, (code, term) in enumerate(zip(codes, terms)):
            target = (code >> 7) & 7
            sums[jnp.where(q * GROUP + k < total, target, BR * KC)] += term

    lax.fori_loop(0, lax.div(total + GROUP - 1, GROUP), multiply, None)


def home_kernel(items, lefts, held, sums):
    sums[...] = jnp.zeros_like(sums)
    run_items(items, lefts, held, 0, sums)


def away_kernel(items, scale, lefts, rights, begun, mine, out, sums, sems):
    sums[...] = begun[...]
    run_items(items, lefts, rights, rights.shape[0] // NX, sums)
    twice = scale[0]

    def store(o):
        return pltpu.make_async_copy(sums.at[o], out.at[o], sems.at[o])

    for o in range(BR * KC):
        value = sums[o]
        sums[o] = value + twice * (mine[o].astype(jnp.float32) - value)
        store(o).start()
    for o in range(BR * KC):
        store(o).wait()


def items_call(kernel, name, in_specs, out_spec, size, scratch):
    return pl.pallas_call(
        kernel,
        out_shape=jax.ShapeDtypeStruct((size, BS, BS), jnp.float32),
        in_specs=in_specs,
        out_specs=out_spec,
        scratch_shapes=scratch,
        compiler_params=pltpu.CompilerParams(vmem_limit_bytes=24 * 1024 * 1024),
        cost_estimate=pl.CostEstimate(
            flops=2 * 16 * BS**3, bytes_accessed=6 << 20, transcendentals=0
        ),
        name=name,
    )


def home_products(items, lefts, held):
    call = items_call(home_kernel, "home", [SMEM] + [VMEM] * 2, VMEM, SUMS, [])
    return call(items, lefts, held)


def away_products(items, scale, lefts, rights, begun, mine):
    scratch = [
        pltpu.VMEM((SUMS, BS, BS), jnp.float32),
        pltpu.SemaphoreType.DMA((BR * KC,)),
    ]
    specs = [SMEM] * 2 + [VMEM] * 4
    out_spec = pl.BlockSpec(memory_space=pltpu.HBM)
    call = items_call(away_kernel, "away", specs, out_spec, BR * KC, scratch)
    return call(items, scale, lefts, rights, begun, mine)


def compact(wanted, places, codes, slots):
    hit = wanted[..., None, :] & (places[..., None, :] == jnp.arange(slots)[:, None])
    return jnp.sum(jnp.where(hit, codes[..., None, :], 0), axis=-1)


def places_of(wanted):
    size = wanted.shape[-1]
    before = jnp.arange(size)[None, :] < jnp.arange(size)[:, None]
    return jnp.sum((wanted[..., None, :] & before).astype(jnp.int32), axis=-1)


def lookup(index, table):
    chosen = index[:, None] == jnp.arange(table.shape[0], dtype=jnp.int32)[None, :]
    found = jnp.dot(
        chosen.astype(jnp.bfloat16),
        table.astype(jnp.bfloat16),
        preferred_element_type=jnp.float32,
    )
    return found.astype(jnp.int32)


def plan(pattern, z, x, y, core):
    col = y * NCORE + core
    plane = lax.dynamic_slice_in_dim(pattern, z * NX * BR, NX * BR, 0)
    group = lax.dynamic_slice_in_dim(pattern, col * KC, KC, 1)
    targets = lax.dynamic_slice_in_dim(plane, col * KC, KC, 1)
    named = lookup(plane.reshape(-1), group).reshape(NX * BR, SLOTS, KC)
    match = (
        (named[..., None] == targets[:, None, None, :])
        & (plane >= 0)[:, :, None, None]
        & (targets >= 0)[:, None, None, :]
    )
    need = jnp.any(match, axis=-1).reshape(NX, BR * SLOTS, KC)
    refs = plane.reshape(NX, BR * SLOTS)
    owner = jnp.where(refs >= 0, refs // BR, -1)
    hit = owner[:, :, None] == jnp.arange(NZ * NX, dtype=jnp.int32)
    table = jnp.stack(
        [jnp.any(hit & need[:, :, u : u + 1], axis=1) for u in range(KC)], axis=-1
    )
    within = jnp.max(jnp.where(hit, (refs % BR)[:, :, None], 0), axis=1)
    table = table.reshape(NX, NZ, NX, KC).transpose(0, 2, 1, 3).reshape(NX, NX, FULL)
    within = within.reshape(NX, NZ, NX).transpose(0, 2, 1)
    place = places_of(table)
    counts = jnp.sum(table.astype(jnp.int32), axis=-1)
    apart = jnp.arange(NX)[:, None] != jnp.arange(NX)[None, :]
    most = jnp.max(jnp.where(apart, counts, 0))

    zs = jnp.arange(NZ, dtype=jnp.int32)[None, :, None]
    us = jnp.arange(KC, dtype=jnp.int32)[None, None, :]
    own_table = lax.dynamic_index_in_dim(table, x, 1, False)
    own_place = lax.dynamic_index_in_dim(place, x, 1, False)
    own_within = lax.dynamic_index_in_dim(within, x, 1, False)
    own_counts = lax.dynamic_index_in_dim(counts, x, 1, False)
    codes = (zs * BR + own_within[:, :, None]) * KC + us
    sends = compact(own_table, own_place, codes.reshape(NX, FULL), FULL)
    send_counts = jnp.where(jnp.arange(NX) == x, 0, own_counts)

    my_refs = lax.dynamic_index_in_dim(refs, x, 0, False)
    my_match = lax.dynamic_slice_in_dim(match, x * BR, BR, 0)
    my_place = lax.dynamic_index_in_dim(place, x, 0, False)
    my_place = my_place.reshape(NX, NZ, KC).transpose(1, 0, 2).reshape(NZ * NX, KC)
    my_owner = jnp.maximum(my_refs, 0) // BR
    there = lookup(my_owner, my_place)
    from_x = my_owner % NX
    us = jnp.arange(KC, dtype=jnp.int32)[None, :]
    at_home = ((my_owner // NX * BR + my_refs % BR) * KC)[:, None] + us
    away = from_x != x
    source = jnp.where(away[:, None], from_x[:, None] * 128 + there, at_home)
    slot = jnp.arange(SLOTS, dtype=jnp.int32)
    rows = jnp.arange(BR, dtype=jnp.int32)[:, None]
    left = ((slot // KC)[None, :] * BR + rows) * KC + (slot % KC)[None, :]
    wanted = jnp.any(my_match, axis=-1)
    aim = rows[:, :, None] * KC + my_match[..., 1].astype(jnp.int32)
    code = left[:, :, None] + 128 * aim + 1024 * source.reshape(BR, SLOTS, KC)
    wanted = wanted & jnp.stack([~away, away]).reshape(2, BR, SLOTS, 1)
    wanted = wanted.reshape(2, ITEMS)
    items = compact(wanted, places_of(wanted), code.reshape(1, ITEMS), ITEMS)
    totals = jnp.sum(wanted.astype(jnp.int32), axis=-1)
    sends = jnp.concatenate([sends.reshape(-1), send_counts])
    items = jnp.concatenate([items, totals[:, None]], axis=1)
    return sends, items, most, targets


def shards(pattern, matrix, atom_set, atom_slab, atom_offset):
    z, x = lax.axis_index("z"), lax.axis_index("x")
    y, core = lax.axis_index("y"), lax.axis_index("core")
    row = z * NX + x
    col = y * NCORE + core
    held = lax.all_gather(matrix, "z", axis=0, tiled=True)
    held = held.reshape(NZ * BR * KC, BS, BS)

    sends, items, most, plane_targets = plan(pattern, z, x, y, core)
    targets = lax.dynamic_slice_in_dim(plane_targets, x * BR, BR, 0)

    own_ids = row * BR + jnp.arange(BR, dtype=jnp.int32)
    on_diag = targets == own_ids[:, None]
    keep = on_diag[:, :, None, None] & jnp.eye(BS, dtype=bool)
    own_diag = jnp.sum(jnp.where(keep, matrix.astype(jnp.float32), 0.0), axis=(1, 2))
    sets = BS // ORB
    gather_sets = (
        jnp.arange(BS)[:, None] // ORB == jnp.arange(sets)[None, :]
    ).astype(jnp.float32)
    set_part = jnp.dot(own_diag, gather_sets, precision=lax.Precision.HIGHEST)
    set_charge = jnp.sum(everyone(set_part.reshape(1, -1), COL), axis=0)[0]
    blocks, set_charge = lax.optimization_barrier((matrix, set_charge))
    lefts = everyone(blocks, COL).reshape(SLOTS * BR, BS, BS)

    atoms_here = atom_set.shape[0]
    find = (
        atom_set[:, None] - row * atoms_here
        == jnp.arange(atoms_here, dtype=jnp.int32)[None, :]
    ).astype(jnp.float32)
    charge = jnp.dot(find, set_charge, precision=lax.Precision.HIGHEST)
    start_x = atom_slab.astype(jnp.float32) * PLANES + atom_offset[0]
    packed = jnp.stack([charge, start_x, atom_offset[1], atom_offset[2]])
    packed = lax.all_gather(everyone(packed, "x"), "z", axis=0, tiled=False)
    packed = packed.reshape(NZ * NX, 4, atoms_here)
    trace = jnp.sum(packed[:, 0])
    weight = jax.nn.sigmoid(sharpness * (half_fill - trace / (NB * BS)))
    scale = (2.0 * weight).reshape(1)
    packed = jnp.concatenate([packed[-2:], packed, packed[:2]])
    near = lax.dynamic_slice_in_dim(packed, row, 5, 0)
    near = near.transpose(1, 0, 2).reshape(4, 5 * atoms_here)

    x_cells = (row * PLANES + jnp.arange(PLANES, dtype=jnp.int32)).astype(jnp.float32)
    y_cells = (col * YC + jnp.arange(YC, dtype=jnp.int32)).astype(jnp.float32)
    z_cells = jnp.arange(GZ, dtype=jnp.int32).astype(jnp.float32)
    density = collocate(
        near, x_cells, y_cells, z_cells, PLANES * NZ * NX, YC * NY * NCORE, GZ
    )

    mine = matrix.reshape(BR * KC, BS, BS)
    sends, lefts, density = lax.optimization_barrier((sends, lefts, density))

    def with_slots(cap):
        def run(sends, items, scale, lefts, held, mine):
            rights = exchange(select(sends, held, cap), "x").reshape(-1, BS, BS)
            begun = home_products(items[0], lefts, held)
            return away_products(items[1], scale, lefts, rights, begun, mine)

        return run

    size = sum((most > cap).astype(jnp.int32) for cap in CAPS[:-1])
    purified = lax.switch(
        size, [with_slots(cap) for cap in CAPS], sends, items, scale, lefts, held, mine
    )
    return purified.reshape(matrix.shape), density


def solution(mesh):
    fine = Mesh(mesh.devices.reshape(NZ, NX, NY, NCORE), (*ROW, *COL))
    placed = (P(), P(ROW, COL, None, None), P(ROW), P(ROW), P(None, ROW))
    return jax.shard_map(
        shards,
        mesh=fine,
        in_specs=placed,
        out_specs=(P(ROW, COL, None, None), P(ROW, COL, None)),
        check_vma=False,
    )
```

```python
import jax
import jax.numpy as jnp
from jax import lax
from jax.experimental import pallas as pl
from jax.experimental.pallas import tpu as pltpu
from jax.sharding import Mesh, PartitionSpec as P

ORB = 8
PLANES = 4
YC = 80
GZ = 640
NZ, NX, NY, NCORE = 16, 4, 4, 2
BR, KC, SLOTS, BS, NB = 4, 2, 16, 128, 256
CAPS = (4, 5, 6, 7, 8, 9, 10, 11, 12, 16, 24, 32)
FULL = NZ * KC
ITEMS = BR * SLOTS * KC
GROUP = 8
SUMS = BR * KC + 1
ROW = ("z", "x")
COL = ("y", "core")

sharpness = 64.0
half_fill = 0.5


def exchange(value, axis):
    return lax.all_to_all(value, axis, split_axis=0, concat_axis=0, tiled=True)


def everyone(value, axis):
    count = lax.axis_size(axis)
    spread = jnp.broadcast_to(value[None], (count, *value.shape))
    return exchange(spread, axis)


def window(delta, length):
    folded = jnp.mod(delta + 0.5 * length, length) - 0.5 * length
    inside = jnp.maximum(1.0 - folded / PLANES * (folded / PLANES), 0.0)
    return inside * inside


def collocate(near, x_cells, y_cells, z_cells, length_x, length_y, length_z):
    along_x = window(x_cells[None, :] - near[1][:, None], length_x)
    along_y = window(y_cells[None, :] - near[2][:, None], length_y)
    along_z = window(z_cells[None, :] - near[3][:, None], length_z)
    plane = near[0][:, None, None] * along_x[:, :, None] * along_y[:, None, :]
    plane = plane.reshape(near.shape[1], x_cells.shape[0] * y_cells.shape[0])
    dense = jnp.dot(plane.T, along_z, precision=lax.Precision.HIGHEST)
    return dense.reshape(x_cells.shape[0], y_cells.shape[0], z_cells.shape[0])


SMEM = pl.BlockSpec(memory_space=pltpu.SMEM)
ANYWHERE = pl.BlockSpec(memory_space=pl.ANY)
VMEM = pl.BlockSpec(memory_space=pltpu.VMEM)


def select_kernel(codes, held, out, stage, in_sems, out_sems):
    def fetch(d, j):
        return pltpu.make_async_copy(
            held.at[codes[d * FULL + j]], stage.at[d, j], in_sems.at[d, j]
        )

    def store(d, j):
        return pltpu.make_async_copy(stage.at[d, j], out.at[d, j], out_sems.at[d, j])

    def pass_on(d, j):
        fetch(d, j).wait()
        store(d, j).start()

    fills = [jnp.minimum(codes[NX * FULL + d], out.shape[1]) for d in range(NX)]
    for d in range(NX):
        lax.fori_loop(0, fills[d], lambda j, _, d=d: fetch(d, j).start(), None)
    for d in range(NX):
        lax.fori_loop(0, fills[d], lambda j, _, d=d: pass_on(d, j), None)
    for d in range(NX):
        lax.fori_loop(0, fills[d], lambda j, _, d=d: store(d, j).wait(), None)


def select(codes, held, cap):
    return pl.pallas_call(
        select_kernel,
        out_shape=jax.ShapeDtypeStruct((NX, cap, BS, BS), jnp.bfloat16),
        in_specs=[SMEM, ANYWHERE],
        out_specs=ANYWHERE,
        scratch_shapes=[
            pltpu.VMEM((NX, cap, BS, BS), jnp.bfloat16),
            pltpu.SemaphoreType.DMA((NX, cap)),
            pltpu.SemaphoreType.DMA((NX, cap)),
        ],
        name="select",
    )(codes, held)


def run_items(items, lefts, rights, stride, sums):
    total = items[ITEMS]

    def multiply(q, _):
        codes = [items[q * GROUP + k] for k in range(GROUP)]
        terms = [
            jnp.dot(
                lefts[code & 127],
                rights[((code >> 10) & 127) + (code >> 17) * stride],
                preferred_element_type=jnp.float32,
            )
            for code in codes
        ]
        for k, (code, term) in enumerate(zip(codes, terms)):
            target = (code >> 7) & 7
            sums[jnp.where(q * GROUP + k < total, target, BR * KC)] += term

    lax.fori_loop(0, lax.div(total + GROUP - 1, GROUP), multiply, None)


def home_kernel(items, lefts, held, sums):
    sums[...] = jnp.zeros_like(sums)
    run_items(items, lefts, held, 0, sums)


def away_kernel(items, scale, lefts, rights, begun, mine, out, sums):
    sums[...] = begun[...]
    run_items(items, lefts, rights, rights.shape[0] // NX, sums)
    twice = scale[0]
    for o in range(BR * KC):
        value = sums[o]
        out[o] = value + twice * (mine[o].astype(jnp.float32) - value)


def items_call(kernel, name, in_specs, out_spec, size, scratch):
    return pl.pallas_call(
        kernel,
        out_shape=jax.ShapeDtypeStruct((size, BS, BS), jnp.float32),
        in_specs=in_specs,
        out_specs=out_spec,
        scratch_shapes=scratch,
        compiler_params=pltpu.CompilerParams(vmem_limit_bytes=24 * 1024 * 1024),
        cost_estimate=pl.CostEstimate(
            flops=2 * 16 * BS**3, bytes_accessed=6 << 20, transcendentals=0
        ),
        name=name,
    )


def home_products(items, lefts, held):
    call = items_call(home_kernel, "home", [SMEM] + [VMEM] * 2, VMEM, SUMS, [])
    return call(items, lefts, held)


def away_products(items, scale, lefts, rights, begun, mine):
    sums = pltpu.VMEM((SUMS, BS, BS), jnp.float32)
    specs = [SMEM] * 2 + [VMEM] * 4
    call = items_call(away_kernel, "away", specs, VMEM, BR * KC, [sums])
    return call(items, scale, lefts, rights, begun, mine)


def compact(wanted, places, codes, slots):
    hit = wanted[..., None, :] & (places[..., None, :] == jnp.arange(slots)[:, None])
    return jnp.sum(jnp.where(hit, codes[..., None, :], 0), axis=-1)


def places_of(wanted):
    size = wanted.shape[-1]
    before = jnp.arange(size)[None, :] < jnp.arange(size)[:, None]
    return jnp.sum((wanted[..., None, :] & before).astype(jnp.int32), axis=-1)


def lookup(index, table):
    chosen = index[:, None] == jnp.arange(table.shape[0], dtype=jnp.int32)[None, :]
    found = jnp.dot(
        chosen.astype(jnp.bfloat16),
        table.astype(jnp.bfloat16),
        preferred_element_type=jnp.float32,
    )
    return found.astype(jnp.int32)


def plan(pattern, z, x, y, core):
    col = y * NCORE + core
    plane = lax.dynamic_slice_in_dim(pattern, z * NX * BR, NX * BR, 0)
    group = lax.dynamic_slice_in_dim(pattern, col * KC, KC, 1)
    targets = lax.dynamic_slice_in_dim(plane, col * KC, KC, 1)
    named = lookup(plane.reshape(-1), group).reshape(NX * BR, SLOTS, KC)
    match = (
        (named[..., None] == targets[:, None, None, :])
        & (plane >= 0)[:, :, None, None]
        & (targets >= 0)[:, None, None, :]
    )
    need = jnp.any(match, axis=-1).reshape(NX, BR * SLOTS, KC)
    refs = plane.reshape(NX, BR * SLOTS)
    owner = jnp.where(refs >= 0, refs // BR, -1)
    hit = owner[:, :, None] == jnp.arange(NZ * NX, dtype=jnp.int32)
    table = jnp.stack(
        [jnp.any(hit & need[:, :, u : u + 1], axis=1) for u in range(KC)], axis=-1
    )
    within = jnp.max(jnp.where(hit, (refs % BR)[:, :, None], 0), axis=1)
    table = table.reshape(NX, NZ, NX, KC).transpose(0, 2, 1, 3).reshape(NX, NX, FULL)
    within = within.reshape(NX, NZ, NX).transpose(0, 2, 1)
    place = places_of(table)
    counts = jnp.sum(table.astype(jnp.int32), axis=-1)
    apart = jnp.arange(NX)[:, None] != jnp.arange(NX)[None, :]
    most = jnp.max(jnp.where(apart, counts, 0))

    zs = jnp.arange(NZ, dtype=jnp.int32)[None, :, None]
    us = jnp.arange(KC, dtype=jnp.int32)[None, None, :]
    own_table = lax.dynamic_index_in_dim(table, x, 1, False)
    own_place = lax.dynamic_index_in_dim(place, x, 1, False)
    own_within = lax.dynamic_index_in_dim(within, x, 1, False)
    own_counts = lax.dynamic_index_in_dim(counts, x, 1, False)
    codes = (zs * BR + own_within[:, :, None]) * KC + us
    sends = compact(own_table, own_place, codes.reshape(NX, FULL), FULL)
    send_counts = jnp.where(jnp.arange(NX) == x, 0, own_counts)

    my_refs = lax.dynamic_index_in_dim(refs, x, 0, False)
    my_match = lax.dynamic_slice_in_dim(match, x * BR, BR, 0)
    my_place = lax.dynamic_index_in_dim(place, x, 0, False)
    my_place = my_place.reshape(NX, NZ, KC).transpose(1, 0, 2).reshape(NZ * NX, KC)
    my_owner = jnp.maximum(my_refs, 0) // BR
    there = lookup(my_owner, my_place)
    from_x = my_owner % NX
    us = jnp.arange(KC, dtype=jnp.int32)[None, :]
    at_home = ((my_owner // NX * BR + my_refs % BR) * KC)[:, None] + us
    away = from_x != x
    source = jnp.where(away[:, None], from_x[:, None] * 128 + there, at_home)
    slot = jnp.arange(SLOTS, dtype=jnp.int32)
    rows = jnp.arange(BR, dtype=jnp.int32)[:, None]
    left = ((slot // KC)[None, :] * BR + rows) * KC + (slot % KC)[None, :]
    wanted = jnp.any(my_match, axis=-1)
    aim = rows[:, :, None] * KC + my_match[..., 1].astype(jnp.int32)
    code = left[:, :, None] + 128 * aim + 1024 * source.reshape(BR, SLOTS, KC)
    wanted = wanted & jnp.stack([~away, away]).reshape(2, BR, SLOTS, 1)
    wanted = wanted.reshape(2, ITEMS)
    items = compact(wanted, places_of(wanted), code.reshape(1, ITEMS), ITEMS)
    totals = jnp.sum(wanted.astype(jnp.int32), axis=-1)
    sends = jnp.concatenate([sends.reshape(-1), send_counts])
    items = jnp.concatenate([items, totals[:, None]], axis=1)
    return sends, items, most, targets


def shards(pattern, matrix, atom_set, atom_slab, atom_offset):
    z, x = lax.axis_index("z"), lax.axis_index("x")
    y, core = lax.axis_index("y"), lax.axis_index("core")
    row = z * NX + x
    col = y * NCORE + core
    held = lax.all_gather(matrix, "z", axis=0, tiled=True)
    held = held.reshape(NZ * BR * KC, BS, BS)

    sends, items, most, plane_targets = plan(pattern, z, x, y, core)
    targets = lax.dynamic_slice_in_dim(plane_targets, x * BR, BR, 0)

    own_ids = row * BR + jnp.arange(BR, dtype=jnp.int32)
    on_diag = targets == own_ids[:, None]
    keep = on_diag[:, :, None, None] & jnp.eye(BS, dtype=bool)
    own_diag = jnp.sum(jnp.where(keep, matrix.astype(jnp.float32), 0.0), axis=(1, 2))
    sets = BS // ORB
    gather_sets = (
        jnp.arange(BS)[:, None] // ORB == jnp.arange(sets)[None, :]
    ).astype(jnp.float32)
    set_part = jnp.dot(own_diag, gather_sets, precision=lax.Precision.HIGHEST)
    set_charge = jnp.sum(everyone(set_part.reshape(1, -1), COL), axis=0)[0]
    blocks, set_charge = lax.optimization_barrier((matrix, set_charge))
    lefts = everyone(blocks, COL).reshape(SLOTS * BR, BS, BS)

    atoms_here = atom_set.shape[0]
    find = (
        atom_set[:, None] - row * atoms_here
        == jnp.arange(atoms_here, dtype=jnp.int32)[None, :]
    ).astype(jnp.float32)
    charge = jnp.dot(find, set_charge, precision=lax.Precision.HIGHEST)
    start_x = atom_slab.astype(jnp.float32) * PLANES + atom_offset[0]
    packed = jnp.stack([charge, start_x, atom_offset[1], atom_offset[2]])
    packed = lax.all_gather(everyone(packed, "x"), "z", axis=0, tiled=False)
    packed = packed.reshape(NZ * NX, 4, atoms_here)
    trace = jnp.sum(packed[:, 0])
    weight = jax.nn.sigmoid(sharpness * (half_fill - trace / (NB * BS)))
    scale = (2.0 * weight).reshape(1)
    packed = jnp.concatenate([packed[-2:], packed, packed[:2]])
    near = lax.dynamic_slice_in_dim(packed, row, 5, 0)
    near = near.transpose(1, 0, 2).reshape(4, 5 * atoms_here)

    x_cells = (row * PLANES + jnp.arange(PLANES, dtype=jnp.int32)).astype(jnp.float32)
    y_cells = (col * YC + jnp.arange(YC, dtype=jnp.int32)).astype(jnp.float32)
    z_cells = jnp.arange(GZ, dtype=jnp.int32).astype(jnp.float32)
    density = collocate(
        near, x_cells, y_cells, z_cells, PLANES * NZ * NX, YC * NY * NCORE, GZ
    )

    mine = matrix.reshape(BR * KC, BS, BS)
    sends, lefts, density = lax.optimization_barrier((sends, lefts, density))

    def with_slots(cap):
        def run(sends, items, scale, lefts, held, mine):
            rights = exchange(select(sends, held, cap), "x").reshape(-1, BS, BS)
            begun = home_products(items[0], lefts, held)
            return away_products(items[1], scale, lefts, rights, begun, mine)

        return run

    size = sum((most > cap).astype(jnp.int32) for cap in CAPS[:-1])
    purified = lax.switch(
        size, [with_slots(cap) for cap in CAPS], sends, items, scale, lefts, held, mine
    )
    return purified.reshape(matrix.shape), density


def solution(mesh):
    fine = Mesh(mesh.devices.reshape(NZ, NX, NY, NCORE), (*ROW, *COL))
    placed = (P(), P(ROW, COL, None, None), P(ROW), P(ROW), P(None, ROW))
    return jax.shard_map(
        shards,
        mesh=fine,
        in_specs=placed,
        out_specs=(P(ROW, COL, None, None), P(ROW, COL, None)),
        check_vma=False,
    )
```
